32 devices in a mesh: pix: 8 (over y, x, core), site: 4 (over z).
Axes of the slice: x: 2, y: 2, z: 4, core: 2. Of those that a mesh axis runs over, the one named last changes fastest.
Arguments:
- margins: int32 [128, 256, 512], P('pix', None, 'site'), may hold values from -2047 to 2047
- block_pos: int32 [128, 4], P('pix', 'site'), may hold values from -1 to 15, as said below
- pattern_ids: int32 [512], P('site'), may hold values from 0 to 15
- pattern_gain: float32 [16, 256], replicated, may hold values from -4 to 4
- site_price: float32 [512], P('site'), may hold values from 0.2 to 4
- weights: float32 [32768], P('pix'), may hold values from 0.2 to 2
- site_start: float32 [512], P('site'), may hold values from 0 to 1
- pixel_start: float32 [32768], P('pix'), may hold values from 0 to 1
- dual_start: float32 [32768], P('pix'), may hold values from 0 to 2
Outputs:
- site_level: float32 [512], P('site')
- pixel_level: float32 [32768], P('pix')
- duals: float32 [32768], P('pix')
The draws below stay inside these ranges and needn't reach their ends.
Inputs may be any that keep to these rules, and one draw needn't show every extreme that they name: Row k of block_pos and of margins is held by pixel device k // 16 and belongs to pixel device (k // 2) % 8; its entry for site block b is the position, among that device's 16 pixel blocks, of the pixel block of the tile, or -1 for an empty slot. The lists are filled unevenly. For one pixel device, drawn afresh, every slot that belongs to it is filled in every row group and site block.
All inputs are finite; a program needn't handle non-finite values.
Results may differ from the reference program's by a relative error of at most 0.0003.
Values may be sent and summed in bfloat16 or wider, within the bound.
A program may use at most 64 MiB of HBM per device.

```python
import math
import jax
import jax.numpy as jnp
from jax import lax

PB_DEV = 16
PIXB = 256
SITEB = 128
CAP = 2
NPAT = 16
ITERS = 2
PIXELS = 32768
SITES = 512
SLOTS = 128
N_PIX = 8
N_SITE = 4


def draw_block_pos(key, part):
    key = jax.random.fold_in(key, 4099)
    key_roll, key_pos, key_star = jax.random.split(key, 3)
    slot = jnp.arange(SLOTS, dtype=jnp.int32)[:, None]
    column = jnp.arange(N_SITE, dtype=jnp.int32)[None, :]
    per_source = N_PIX * CAP
    source = slot // per_source
    target = slot % per_source // CAP
    within = slot % CAP
    pix_span = max(N_PIX - 1, 1)
    site_span = max(N_SITE - 1, 1)
    denom = 2 * pix_span * site_span
    roll = jax.random.randint(key_roll, (SLOTS, N_SITE), 0, 10 * denom, dtype=jnp.int32)
    filled = roll < 3 * denom + 3 * ((source + target) * site_span + 2 * column * pix_span)
    chosen = jax.random.randint(key_star, (), 0, N_PIX, dtype=jnp.int32)
    filled = filled | (target == chosen)
    position = jax.random.randint(key_pos, (SLOTS, N_SITE), 0, PB_DEV, dtype=jnp.int32)
    result = jnp.where(filled, position, -1)
    leading = (source == 0) & (within == 0) & (column == 0)
    result = jnp.where(leading & (target == chosen), PB_DEV - 1, result)
    result = jnp.where(leading & (target == (chosen + 1) % N_PIX), -1, result)
    return result.astype(jnp.int32)


def set_ends(array, key, smallest, top_value):
    spot = [jax.random.randint(jax.random.fold_in(key, axis), (), 0, length) for axis, length in enumerate(array.shape)]
    longest = array.shape.index(max(array.shape))
    next_to = spot[:longest] + [(spot[longest] + 1) % array.shape[longest]] + spot[longest + 1:]
    return array.at[tuple(spot)].set(smallest).at[tuple(next_to)].set(top_value)


def block_levels(stream_key, extent, cuts, low, high):
    factor_of = 1.0
    for dim, parts in cuts:
        steps = jax.random.uniform(jax.random.fold_in(jax.random.fold_in(stream_key, 6), dim), (parts,), jnp.float32, low / len(cuts), high / len(cuts))
        factor_of = factor_of * jnp.repeat(jnp.exp(steps), extent[dim] // parts).reshape((-1,) + (1,) * (len(extent) - 1 - dim))
    return factor_of


def centred(rng, extent, scale, most, held_as=jnp.bfloat16):
    values = jax.random.normal(rng, extent, jnp.float32) * scale
    return jnp.minimum(jnp.maximum(values, -most), most).astype(held_as)


def setup_inputs(seed: int = 0) -> dict:
    streams_of = jax.random.split(jax.random.key(seed), 10)
    return {
        "margins": set_ends(jax.random.randint(streams_of[0], (SLOTS, PIXB, SITES), -2047, 2048), jax.random.fold_in(streams_of[0], 1), -2047, 2047).astype(jnp.int32),
        "block_pos": draw_block_pos(jax.random.fold_in(streams_of[9], 71), 0),
        "pattern_ids": set_ends(jax.random.randint(streams_of[2], (SITES,), 0, NPAT), jax.random.fold_in(streams_of[2], 1), 0, NPAT - 1).astype(jnp.int32),
        "pattern_gain": centred(streams_of[3], (NPAT, PIXB), 1.0, 4.0, jnp.float32),
        "site_price": jnp.clip(jnp.exp(math.log(4.0) - 2.9957323 * jax.random.uniform(streams_of[4], (SITES,), jnp.float32) ** block_levels(streams_of[4], (SITES,), ((0, 4),), -0.2, 0.2)), 0.2, 4.0),
        "weights": jnp.clip(jnp.exp(math.log(2.0) - 2.3025851 * jax.random.uniform(streams_of[5], (PIXELS,), jnp.float32) ** block_levels(streams_of[5], (PIXELS,), ((0, 8),), -0.2, 0.2)), 0.2, 2.0),
        "site_start": jnp.clip(1.0 * jax.random.uniform(streams_of[6], (SITES,), jnp.float32) ** block_levels(streams_of[6], (SITES,), ((0, 4),), -0.2, 0.2), 0.0, 1.0),
        "pixel_start": jnp.clip(1.0 * jax.random.uniform(streams_of[7], (PIXELS,), jnp.float32) ** block_levels(streams_of[7], (PIXELS,), ((0, 8),), -0.2, 0.2), 0.0, 1.0),
        "dual_start": jnp.clip(2.0 * jax.random.uniform(streams_of[8], (PIXELS,), jnp.float32) ** block_levels(streams_of[8], (PIXELS,), ((0, 8),), -0.2, 0.2), 0.0, 2.0),
    }


MARGIN_SCALE = 2.0 ** -9


def build_tiles(margin_rows, positions, gain_tile):
    filled = jnp.repeat(positions >= 0, SITEB, axis=1)
    values = jax.nn.sigmoid(margin_rows.astype(jnp.float32) * MARGIN_SCALE + gain_tile[None])
    return jnp.where(filled[:, None, :], values, 0.0).astype(jnp.bfloat16)


def block_index(positions):
    target = jnp.arange(N_PIX * CAP, dtype=jnp.int32) // CAP
    return jnp.where(positions >= 0, target[:, None] * PB_DEV + positions, 0).astype(jnp.int32)


def apply_transpose(margin_groups, position_groups, gain_tile, dual_half):
    def absorb(running, pieces):
        margin_rows, positions = pieces
        coverage = build_tiles(margin_rows, positions, gain_tile).astype(jnp.float32)
        coverage = coverage.reshape(coverage.shape[0], PIXB, N_SITE, SITEB)
        picked = dual_half[block_index(positions)].astype(jnp.float32)
        partial_value = jnp.einsum("kbr,krbj->bj", picked, coverage, precision=lax.Precision.HIGHEST)
        return running + partial_value.reshape(SITES), None

    running, unused = lax.scan(absorb, jnp.zeros((SITES,), jnp.float32), (margin_groups, position_groups))
    return running


def apply_forward(margin_groups, position_groups, gain_tile, site_half):
    spread = site_half.astype(jnp.float32).reshape(N_SITE, SITEB)

    def absorb(running, pieces):
        margin_rows, positions = pieces
        coverage = build_tiles(margin_rows, positions, gain_tile).astype(jnp.float32)
        coverage = coverage.reshape(coverage.shape[0], PIXB, N_SITE, SITEB)
        products = jnp.einsum("krbj,bj->kbr", coverage, spread, precision=lax.Precision.HIGHEST)
        running = running.at[block_index(positions).reshape(-1)].add(products.reshape(-1, PIXB))
        return running, None

    running, unused = lax.scan(absorb, jnp.zeros((PB_DEV * N_PIX, PIXB), jnp.float32), (margin_groups, position_groups))
    return running.reshape(PIXELS)


def reference(margins, block_pos, pattern_ids, pattern_gain, site_price, weights, site_start, pixel_start, dual_start):
    gain_tile = pattern_gain[pattern_ids].T
    margin_groups = margins.reshape(N_PIX, N_PIX * CAP, PIXB, SITES)
    position_groups = block_pos.reshape(N_PIX, N_PIX * CAP, N_SITE)
    ones_pixels = jnp.ones((PB_DEV * N_PIX, PIXB), jnp.bfloat16)
    column_sum = apply_transpose(margin_groups, position_groups, gain_tile, ones_pixels)
    row_sum = apply_forward(margin_groups, position_groups, gain_tile, jnp.ones((SITES,), jnp.bfloat16))
    site_level, pixel_level, duals = site_start, pixel_start, dual_start
    for iteration in range(ITERS):
        dual_half = duals.astype(jnp.bfloat16).reshape(PB_DEV * N_PIX, PIXB)
        pulled = apply_transpose(margin_groups, position_groups, gain_tile, dual_half)
        new_site = jnp.clip(site_level - (site_price - pulled / column_sum), 0.0, 1.0)
        new_pixel = jnp.clip(pixel_level - (duals - weights), 0.0, 1.0)
        extrapolated = (2.0 * new_site - site_level).astype(jnp.bfloat16)
        pushed = apply_forward(margin_groups, position_groups, gain_tile, extrapolated)
        duals = jnp.maximum(duals + ((2.0 * new_pixel - pixel_level) - pushed) / (row_sum + 1.0), 0.0)
        site_level, pixel_level = new_site, new_pixel
    return site_level, pixel_level, duals
```

```python
import functools

import jax
import jax.numpy as jnp
from jax import lax
from jax.experimental import pallas as pl
from jax.experimental.pallas import tpu as pltpu
from jax.sharding import PartitionSpec as P

ITERS = 2
MARGIN_SCALE = 2.0 ** (-9)
LANES = 128
MESH = pl.DeviceIdType.MESH
NT = (((1,), (1,)), ((), ()))


def kernel(
    npix,
    nsite,
    margins_ref,
    pos_ref,
    ids_ref,
    gain_ref,
    price_ref,
    weights_ref,
    site_ref,
    pixel_ref,
    dual_ref,
    site_out,
    pixel_out,
    dual_out,
    margins_v,
    tiles,
    dual_all,
    row_send,
    row_recv,
    col_recv,
    push_send,
    push_recv,
    level_recv,
    margin_sem,
    dual_sem,
    row_sem,
    col_sem,
    push_sem,
    level_sem,
):
    slots, width, sites = margins_v.shape
    cap = slots // npix
    halves = width // LANES
    rows = dual_ref.shape[0]
    me = lax.axis_index("pix")
    here = lax.axis_index("site")

    def pix_peer(step):
        return lax.rem(me + step, npix)

    def site_peer(step):
        return lax.rem(here + step, nsite)

    def margin_copy(t):
        part = pl.ds(t * cap, cap)
        return pltpu.make_async_copy(margins_ref.at[part], margins_v.at[part], margin_sem.at[t])

    for t in range(npix):
        margin_copy(t).start()

    barrier = pltpu.get_barrier_semaphore()
    for step in range(1, npix):
        pl.semaphore_signal(barrier, inc=1, device_id=(pix_peer(step), here), device_id_type=MESH)
    for step in range(1, nsite):
        pl.semaphore_signal(barrier, inc=1, device_id=(me, site_peer(step)), device_id_type=MESH)

    def send_pix(src, dst, sems, step):
        pltpu.make_async_remote_copy(
            src_ref=src,
            dst_ref=dst,
            send_sem=sems.at[0],
            recv_sem=sems.at[1],
            device_id=(pix_peer(step), here),
            device_id_type=MESH,
        ).start()

    def send_site(src, dst, sems, step):
        pltpu.make_async_remote_copy(
            src_ref=src,
            dst_ref=dst,
            send_sem=sems.at[0],
            recv_sem=sems.at[1],
            device_id=(me, site_peer(step)),
            device_id_type=MESH,
        ).start()

    def drain(buffer, sem):
        part = buffer.at[pl.ds(0, buffer.shape[0] - 1)]
        pltpu.make_async_copy(part, part, sem).wait()

    def share_duals(i, values):
        dual_all[i, pl.ds(me, 1)] = values.astype(jnp.bfloat16)[None]

        def go():
            for step in range(1, npix):
                send_pix(dual_all.at[i, me], dual_all.at[i, me], dual_sem.at[i], step)

        return go

    go = share_duals(0, dual_ref[...])
    pl.semaphore_wait(barrier, npix + nsite - 2)
    go()

    pos = pos_ref[...]
    slot_col = lax.broadcasted_iota(jnp.int32, (slots, 1), 0)
    base = jnp.where(pos >= 0, (slot_col // cap) * rows + pos * halves, -halves)
    row_id = lax.broadcasted_iota(jnp.int32, (slots, npix * rows), 1)
    choosers = [
        (row_id == base + h).astype(jnp.float32).astype(jnp.bfloat16) for h in range(halves)
    ]
    pos_rows = jnp.broadcast_to(pos.astype(jnp.float32), (slots, LANES))
    for t in range(npix):
        row_send[t, halves * cap :, :] = pos_rows[t * cap : (t + 1) * cap]
    filled = jnp.broadcast_to((pos >= 0).astype(jnp.float32), (slots, width))
    slot_row = lax.broadcasted_iota(jnp.int32, (slots, width), 0)
    slot_lane = lax.broadcasted_iota(jnp.int32, (slots, LANES), 0)

    def of_target(t, values):
        return jnp.where(slot_row // cap == t, values, 0.0).astype(jnp.bfloat16)

    def column_fold(sums):
        total = jnp.zeros((1, LANES), jnp.float32)
        for c in range(cap):
            part = sums[:, c * LANES : (c + 1) * LANES]
            total = total + jnp.sum(
                jnp.where(slot_lane % cap == c, part, 0.0), axis=0, keepdims=True
            )
        return total

    lane_row = lax.broadcasted_iota(jnp.int32, (16, cap * LANES), 0)
    lane_cap = lax.broadcasted_iota(jnp.int32, (16, cap * LANES), 1) // LANES

    def spread_sites(values):
        wide = jnp.concatenate([values] * cap, axis=1)
        return jnp.where(lane_row == lane_cap, wide, 0.0).astype(jnp.bfloat16)

    chooser = (
        lax.broadcasted_iota(jnp.int32, (gain_ref.shape[0], sites), 0) == ids_ref[...]
    ).astype(jnp.float32)
    gain_half = 0.5 * lax.dot_general(
        gain_ref[...],
        chooser,
        (((0,), (0,)), ((), ())),
        precision=lax.Precision.HIGHEST,
        preferred_element_type=jnp.float32,
    )
    ones_sites = spread_sites(jnp.ones((1, LANES), jnp.float32))

    def put_rows(buffer, t, products):
        for h in range(halves):
            buffer[t, h * cap : (h + 1) * cap, :] = products[:cap, h * LANES : (h + 1) * LANES]

    def build(t, sums):
        margin_copy(t).wait()
        for c in range(cap):
            values = margins_v[t * cap + c].astype(jnp.float32)
            values = 0.5 * jnp.tanh(values * (0.5 * MARGIN_SCALE) + gain_half) + 0.5
            tiles[t, :, c * LANES : (c + 1) * LANES] = values.astype(jnp.bfloat16)
        tile = tiles[t]
        put_rows(
            row_send,
            t,
            lax.dot_general(ones_sites, tile, NT, preferred_element_type=jnp.float32),
        )
        return sums + jnp.dot(of_target(t, filled), tile, preferred_element_type=jnp.float32)

    column_sums = lax.fori_loop(
        0, npix, build, jnp.zeros((slots, cap * LANES), jnp.float32)
    )
    col_recv[0, pl.ds(me, 1), 1:2] = column_fold(column_sums)[None]

    for step in range(1, npix):
        send_pix(row_send.at[pix_peer(step)], row_recv.at[me], row_sem, step)
    row_recv[pl.ds(me, 1)] = row_send[pl.ds(me, 1)]

    state_row = lax.broadcasted_iota(jnp.int32, (rows, LANES), 0).astype(jnp.float32)

    def gather_rows(buffer):
        total = jnp.zeros((rows, LANES), jnp.float32)
        for s in range(npix):
            for c in range(cap):
                at = row_recv[s, halves * cap + c : halves * cap + c + 1, :] * halves
                for h in range(halves):
                    line = buffer[s, h * cap + c : h * cap + c + 1, :]
                    total = total + jnp.where(state_row == at + h, line, 0.0)
        return total

    def share_levels(i, values):
        level_recv[i, pl.ds(here, 1)] = values[None]
        for step in range(1, nsite):
            send_site(level_recv.at[i, here], level_recv.at[i, here], level_sem.at[i], step)

    def total_levels(i):
        drain(level_recv.at[i], level_sem.at[i, 1])
        total = level_recv[i, 0]
        for z in range(1, nsite):
            total = total + level_recv[i, z]
        return total

    site_level = site_ref[...]
    pixel_level = pixel_ref[...]
    duals = dual_ref[...]
    column_sum = None
    row_sum = None
    for i in range(ITERS):
        drain(dual_all.at[i], dual_sem.at[i, 1])
        all_rows = dual_all[i].reshape(npix * rows, LANES)
        selected = jnp.concatenate(
            [jnp.dot(ch, all_rows, preferred_element_type=jnp.float32) for ch in choosers], axis=1
        )
        sums = jnp.zeros((slots, cap * LANES), jnp.float32)
        for t in range(npix):
            sums = sums + jnp.dot(
                of_target(t, selected), tiles[t], preferred_element_type=jnp.float32
            )
        col_recv[i, pl.ds(me, 1), 0:1] = column_fold(sums)[None]
        for step in range(1, npix):
            send_pix(col_recv.at[i, me], col_recv.at[i, me], col_sem.at[i], step)

        new_pixel = jnp.clip(pixel_level - (duals - weights_ref[...]), 0.0, 1.0)
        ahead = 2.0 * new_pixel - pixel_level
        if i == 0:
            drain(row_recv, row_sem.at[1])
            share_levels(ITERS, gather_rows(row_recv))

        drain(col_recv.at[i], col_sem.at[i, 1])
        pulled = col_recv[i, 0]
        for s in range(1, npix):
            pulled = pulled + col_recv[i, s]
        if i == 0:
            column_sum = pulled[1:2]
        new_site = jnp.clip(site_level - (price_ref[...] - pulled[0:1] / column_sum), 0.0, 1.0)
        ahead_sites = spread_sites(2.0 * new_site - site_level)
        for step in list(range(1, npix)) + [0]:
            t = pix_peer(step)
            put_rows(
                push_send.at[i],
                t,
                lax.dot_general(ahead_sites, tiles[t], NT, preferred_element_type=jnp.float32),
            )
            if step:
                send_pix(push_send.at[i, t], push_recv.at[i, me], push_sem.at[i], step)
        push_recv[i, pl.ds(me, 1)] = push_send[i, pl.ds(me, 1)]
        drain(push_recv.at[i], push_sem.at[i, 1])
        share_levels(i, gather_rows(push_recv.at[i]))
        if i == 0:
            row_sum = total_levels(ITERS)
        pushed = total_levels(i)
        duals = jnp.maximum(duals + (ahead - pushed) / (row_sum + 1.0), 0.0)
        if i < ITERS - 1:
            share_duals(i + 1, duals)()
        site_level, pixel_level = new_site, new_pixel

    site_out[...] = site_level
    pixel_out[...] = pixel_level
    dual_out[...] = duals

    drain(row_recv, row_sem.at[0])
    drain(level_recv.at[ITERS], level_sem.at[ITERS, 0])
    for i in range(ITERS):
        drain(dual_all.at[i], dual_sem.at[i, 0])
        drain(col_recv.at[i], col_sem.at[i, 0])
        drain(push_recv.at[i], push_sem.at[i, 0])
        drain(level_recv.at[i], level_sem.at[i, 0])


def local(
    npix,
    nsite,
    margins,
    block_pos,
    pattern_ids,
    pattern_gain,
    site_price,
    weights,
    site_start,
    pixel_start,
    dual_start,
):
    slots, width, sites = margins.shape
    cap = slots // npix
    halves = width // LANES
    rows = weights.shape[0] // LANES
    f32 = jnp.float32
    whole = pl.BlockSpec(memory_space=pltpu.VMEM)
    dma = pltpu.SemaphoreType.DMA
    site_level, pixel_level, duals = pl.pallas_call(
        functools.partial(kernel, npix, nsite),
        out_shape=(
            jax.ShapeDtypeStruct((1, sites), f32),
            jax.ShapeDtypeStruct((rows, LANES), f32),
            jax.ShapeDtypeStruct((rows, LANES), f32),
        ),
        in_specs=[pl.BlockSpec(memory_space=pl.ANY)] + [whole] * 8,
        out_specs=(whole, whole, whole),
        scratch_shapes=[
            pltpu.VMEM((slots, width, sites), jnp.int32),
            pltpu.VMEM((npix, width, cap * sites), jnp.bfloat16),
            pltpu.VMEM((ITERS, npix, rows, LANES), jnp.bfloat16),
            pltpu.VMEM((npix, (halves + 1) * cap, LANES), f32),
            pltpu.VMEM((npix, (halves + 1) * cap, LANES), f32),
            pltpu.VMEM((ITERS, npix, 2, LANES), f32),
            pltpu.VMEM((ITERS, npix, halves * cap, LANES), f32),
            pltpu.VMEM((ITERS, npix, halves * cap, LANES), f32),
            pltpu.VMEM((ITERS + 1, nsite, rows, LANES), f32),
            dma((npix,)),
            dma((ITERS, 2)),
            dma((2,)),
            dma((ITERS, 2)),
            dma((ITERS, 2)),
            dma((ITERS + 1, 2)),
        ],
        compiler_params=pltpu.CompilerParams(
            collective_id=0, has_side_effects=True, vmem_limit_bytes=40 * 1024 * 1024
        ),
    )(
        margins,
        block_pos,
        pattern_ids.reshape(1, sites),
        pattern_gain,
        site_price.reshape(1, sites),
        weights.reshape(rows, LANES),
        site_start.reshape(1, sites),
        pixel_start.reshape(rows, LANES),
        dual_start.reshape(rows, LANES),
    )
    return site_level.reshape(-1), pixel_level.reshape(-1), duals.reshape(-1)


def solution(mesh):
    placed = (
        P("pix", None, "site"),
        P("pix", "site"),
        P("site"),
        P(),
        P("site"),
        P("pix"),
        P("site"),
        P("pix"),
        P("pix"),
    )
    return jax.shard_map(
        functools.partial(local, mesh.shape["pix"], mesh.shape["site"]),
        mesh=mesh,
        in_specs=placed,
        out_specs=(P("site"), P("pix"), P("pix")),
        check_vma=False,
    )
```

```python
import functools

import jax
import jax.numpy as jnp
from jax import lax
from jax.experimental import pallas as pl
from jax.experimental.pallas import tpu as pltpu
from jax.sharding import PartitionSpec as P

ITERS = 2
MARGIN_SCALE = 2.0 ** (-9)
LANES = 128
MESH = pl.DeviceIdType.MESH


def kernel(
    npix,
    nsite,
    margins_hbm,
    pos_hbm,
    ids_hbm,
    gain_hbm,
    price_hbm,
    weights_hbm,
    site_hbm,
    pixel_hbm,
    dual_hbm,
    site_hbm_out,
    pixel_hbm_out,
    dual_hbm_out,
    site_out,
    pixel_out,
    dual_out,
    margins_v,
    pos_ref,
    ids_ref,
    gain_ref,
    price_ref,
    weights_ref,
    site_ref,
    pixel_ref,
    dual_ref,
    tiles,
    tiles_t,
    dual_all,
    row_send,
    row_recv,
    col_recv,
    push_send,
    push_recv,
    margin_sem,
    small_sem,
    dual_sem,
    row_sem,
    col_sem,
    push_sem,
):
    slots, width, sites = margins_v.shape
    cap = slots // npix
    halves = width // LANES
    rows = dual_ref.shape[0]
    me = lax.axis_index("pix")
    here = lax.axis_index("site")
    mine = here * npix + me

    def pix_peer(step):
        return lax.rem(me + step, npix)

    def site_peer(step):
        return lax.rem(here + step, nsite)

    peers = [(p, z) for z in range(nsite) for p in range(npix) if p or z]

    small = [
        pltpu.make_async_copy(src, dst, small_sem.at[n])
        for n, (src, dst) in enumerate(
            (
                (dual_hbm, dual_ref),
                (pos_hbm, pos_ref),
                (ids_hbm, ids_ref),
                (gain_hbm, gain_ref),
                (price_hbm, price_ref),
                (weights_hbm, weights_ref),
                (site_hbm, site_ref),
                (pixel_hbm, pixel_ref),
            )
        )
    ]

    def margin_copy(t):
        part = pl.ds(t * cap, cap)
        return pltpu.make_async_copy(margins_hbm.at[part], margins_v.at[part], margin_sem.at[t])

    for copy in small:
        copy.start()
    for t in range(npix):
        margin_copy(t).start()

    barrier = pltpu.get_barrier_semaphore()
    for p, z in peers:
        pl.semaphore_signal(
            barrier, inc=1, device_id=(pix_peer(p), site_peer(z)), device_id_type=MESH
        )

    def send(src, dst, sems, p, z):
        pltpu.make_async_remote_copy(
            src_ref=src,
            dst_ref=dst,
            send_sem=sems.at[0],
            recv_sem=sems.at[1],
            device_id=(pix_peer(p), site_peer(z)),
            device_id_type=MESH,
        ).start()

    def drain(buffer, sem):
        part = buffer.at[pl.ds(0, buffer.shape[0] - 1)]
        pltpu.make_async_copy(part, part, sem).wait()

    def share_duals(i, values):
        dual_all[i, pl.ds(me, 1)] = values.astype(jnp.bfloat16)[None]

    def send_duals(i):
        for p in range(1, npix):
            send(dual_all.at[i, me], dual_all.at[i, me], dual_sem.at[i], p, 0)

    for copy in small:
        copy.wait()
    share_duals(0, dual_ref[...])

    diagonal = lax.broadcasted_iota(jnp.int32, (slots, slots), 0) == lax.broadcasted_iota(
        jnp.int32, (slots, slots), 1
    )
    pos = jnp.sum(
        jnp.where(diagonal, pos_ref[...].astype(jnp.float32), 0.0), axis=1, keepdims=True
    )
    slot_col = lax.broadcasted_iota(jnp.int32, (slots, 1), 0)
    first = ((slot_col // cap) * rows).astype(jnp.float32)
    base = jnp.where(pos >= 0.0, first + pos * halves, -1.0 * halves)
    row_id = lax.broadcasted_iota(jnp.int32, (slots, npix * rows), 1).astype(jnp.float32)
    choosers = [
        jnp.where(row_id == base + h, 1.0, 0.0).astype(jnp.bfloat16) for h in range(halves)
    ]
    pos_rows = jnp.broadcast_to(pos, (slots, LANES))
    for t in range(npix):
        row_send[t, halves * cap :, :] = pos_rows[t * cap : (t + 1) * cap]
    filled = jnp.broadcast_to(jnp.where(pos >= 0.0, 1.0, 0.0), (slots, width))
    slot_row = lax.broadcasted_iota(jnp.int32, (slots, width), 0) // cap
    slot_lane = lax.broadcasted_iota(jnp.int32, (slots, LANES), 0) % cap

    def of_target(t, values):
        return jnp.where(slot_row == t, values, 0.0).astype(jnp.bfloat16)

    def column_fold(sums):
        total = jnp.zeros((1, LANES), jnp.float32)
        for c in range(cap):
            part = sums[:, c * LANES : (c + 1) * LANES]
            total = total + jnp.sum(jnp.where(slot_lane == c, part, 0.0), axis=0, keepdims=True)
        return total

    lane_row = lax.broadcasted_iota(jnp.int32, (16, cap * LANES), 0)
    lane_cap = lax.broadcasted_iota(jnp.int32, (16, cap * LANES), 1) // LANES

    def spread_sites(values):
        wide = jnp.concatenate([values] * cap, axis=1)
        return jnp.where(lane_row == lane_cap, wide, 0.0).astype(jnp.bfloat16)

    chooser = (
        lax.broadcasted_iota(jnp.int32, (gain_ref.shape[0], sites), 0) == ids_ref[...]
    ).astype(jnp.float32)
    gain_half = 0.5 * lax.dot_general(
        gain_ref[...],
        chooser,
        (((0,), (0,)), ((), ())),
        precision=lax.Precision.HIGHEST,
        preferred_element_type=jnp.float32,
    )

    pl.semaphore_wait(barrier, len(peers))
    send_duals(0)

    def build(t, carry):
        margin_copy(t).wait()
        for c in range(cap):
            part = slice(c * LANES, (c + 1) * LANES)
            values = margins_v[t * cap + c].astype(jnp.float32)
            values = 0.5 * jnp.tanh(values * (0.5 * MARGIN_SCALE) + gain_half) + 0.5
            values = values.astype(jnp.bfloat16)
            tiles[t, :, part] = values
            tiles_t[t, part, :] = values.T
        return carry

    lax.fori_loop(0, npix, build, 0)

    def send_products(values, source, target, sems):
        lhs = spread_sites(values)
        for t in range(npix):
            products = jnp.dot(lhs, tiles_t[t], preferred_element_type=jnp.float32)
            for h in range(halves):
                source[t, h * cap : (h + 1) * cap, :] = products[
                    :cap, h * LANES : (h + 1) * LANES
                ]
        for p, z in peers:
            send(source.at[pix_peer(p)], target.at[mine], sems, p, z)
        target[pl.ds(mine, 1)] = source[pl.ds(me, 1)]

    state_row = lax.broadcasted_iota(jnp.int32, (rows, LANES), 0).astype(jnp.float32)

    def gather_rows(buffer):
        def group(z, total):
            for p in range(npix):
                s = z * npix + p
                for c in range(cap):
                    line = row_recv[s, halves * cap + c : halves * cap + c + 1, :]
                    offset = state_row - line * halves
                    for h in range(halves):
                        line = buffer[s, h * cap + c : h * cap + c + 1, :]
                        total = total + jnp.where(offset == h, line, 0.0)
            return total

        return lax.fori_loop(0, nsite, group, jnp.zeros((rows, LANES), jnp.float32))

    site_level = site_ref[...]
    pixel_level = pixel_ref[...]
    duals = dual_ref[...]
    column_sum = None
    row_sum = None
    for i in range(ITERS):
        drain(dual_all.at[i], dual_sem.at[i, 1])
        all_rows = dual_all[i].reshape(npix * rows, LANES)
        selected = jnp.concatenate(
            [jnp.dot(ch, all_rows, preferred_element_type=jnp.float32) for ch in choosers], axis=1
        )
        groups = [selected, filled] if i == 0 else [selected]
        sums = jnp.zeros((len(groups) * slots, cap * LANES), jnp.float32)
        for t in range(npix):
            lhs = jnp.concatenate([of_target(t, group) for group in groups], axis=0)
            sums = sums + jnp.dot(lhs, tiles[t], preferred_element_type=jnp.float32)
        for n in range(len(groups)):
            total = column_fold(sums[n * slots : (n + 1) * slots])
            col_recv[i, pl.ds(me, 1), n : n + 1] = total[None]
        for p in range(1, npix):
            send(col_recv.at[i, me], col_recv.at[i, me], col_sem.at[i], p, 0)

        new_pixel = jnp.clip(pixel_level - (duals - weights_ref[...]), 0.0, 1.0)
        ahead = 2.0 * new_pixel - pixel_level
        if i == 0:
            send_products(jnp.ones((1, LANES), jnp.float32), row_send, row_recv, row_sem)

        drain(col_recv.at[i], col_sem.at[i, 1])
        pulled = col_recv[i, 0]
        for s in range(1, npix):
            pulled = pulled + col_recv[i, s]
        if i == 0:
            column_sum = pulled[1:2]
        new_site = jnp.clip(site_level - (price_ref[...] - pulled[0:1] / column_sum), 0.0, 1.0)
        send_products(
            2.0 * new_site - site_level, push_send.at[i], push_recv.at[i], push_sem.at[i]
        )
        if i == 0:
            drain(row_recv, row_sem.at[1])
            row_sum = gather_rows(row_recv) + 1.0
        drain(push_recv.at[i], push_sem.at[i, 1])
        pushed = gather_rows(push_recv.at[i])
        duals = jnp.maximum(duals + (ahead - pushed) / row_sum, 0.0)
        if i < ITERS - 1:
            share_duals(i + 1, duals)
            send_duals(i + 1)
        site_level, pixel_level = new_site, new_pixel

    site_out[...] = site_level
    pixel_out[...] = pixel_level
    dual_out[...] = duals
    write_out(
        site_out, pixel_out, dual_out, site_hbm_out, pixel_hbm_out, dual_hbm_out, small_sem
    )

    drain(row_recv, row_sem.at[0])
    for i in range(ITERS):
        drain(dual_all.at[i], dual_sem.at[i, 0])
        drain(col_recv.at[i], col_sem.at[i, 0])
        drain(push_recv.at[i], push_sem.at[i, 0])


def write_out(site_in, pixel_in, dual_in, site_out, pixel_out, dual_out, sem):
    copies = [
        pltpu.make_async_copy(src, dst, sem.at[n])
        for n, (src, dst) in enumerate(
            ((site_in, site_out), (pixel_in, pixel_out), (dual_in, dual_out))
        )
    ]
    for copy in copies:
        copy.start()
    for copy in copies:
        copy.wait()


def local(
    npix,
    nsite,
    margins,
    block_pos,
    pattern_ids,
    pattern_gain,
    site_price,
    weights,
    site_start,
    pixel_start,
    dual_start,
):
    slots, width, sites = margins.shape
    cap = slots // npix
    halves = width // LANES
    rows = weights.shape[0] // LANES
    devices = npix * nsite
    f32 = jnp.float32
    i32 = jnp.int32
    hbm = pl.BlockSpec(memory_space=pltpu.HBM)
    dma = pltpu.SemaphoreType.DMA
    results = (
        jax.ShapeDtypeStruct((1, sites), f32),
        jax.ShapeDtypeStruct((rows, LANES), f32),
        jax.ShapeDtypeStruct((rows, LANES), f32),
    )
    found = pl.pallas_call(
        functools.partial(kernel, npix, nsite),
        out_shape=results,
        in_specs=[hbm] * 9,
        out_specs=(hbm, hbm, hbm),
        scratch_shapes=[
            pltpu.VMEM((1, sites), f32),
            pltpu.VMEM((rows, LANES), f32),
            pltpu.VMEM((rows, LANES), f32),
            pltpu.VMEM((slots, width, sites), i32),
            pltpu.VMEM((1, slots), i32),
            pltpu.VMEM((1, sites), i32),
            pltpu.VMEM(pattern_gain.shape, f32),
            pltpu.VMEM((1, sites), f32),
            pltpu.VMEM((rows, LANES), f32),
            pltpu.VMEM((1, sites), f32),
            pltpu.VMEM((rows, LANES), f32),
            pltpu.VMEM((rows, LANES), f32),
            pltpu.VMEM((npix, width, cap * sites), jnp.bfloat16),
            pltpu.VMEM((npix, cap * sites, width), jnp.bfloat16),
            pltpu.VMEM((ITERS, npix, rows, LANES), jnp.bfloat16),
            pltpu.VMEM((npix, (halves + 1) * cap, LANES), f32),
            pltpu.VMEM((devices, (halves + 1) * cap, LANES), f32),
            pltpu.VMEM((ITERS, npix, 2, LANES), f32),
            pltpu.VMEM((ITERS, npix, halves * cap, LANES), f32),
            pltpu.VMEM((ITERS, devices, halves * cap, LANES), f32),
            dma((npix,)),
            dma((8,)),
            dma((ITERS, 2)),
            dma((2,)),
            dma((ITERS, 2)),
            dma((ITERS, 2)),
        ],
        compiler_params=pltpu.CompilerParams(
            collective_id=0, has_side_effects=True, vmem_limit_bytes=60 * 1024 * 1024
        ),
    )(
        margins,
        block_pos.reshape(1, slots),
        pattern_ids.reshape(1, sites),
        pattern_gain,
        site_price.reshape(1, sites),
        weights.reshape(rows, LANES),
        site_start.reshape(1, sites),
        pixel_start.reshape(rows, LANES),
        dual_start.reshape(rows, LANES),
    )
    site_level, pixel_level, duals = pl.pallas_call(
        write_out,
        out_shape=results,
        in_specs=[hbm] * 3,
        out_specs=(hbm, hbm, hbm),
        scratch_shapes=[dma((3,))],
        compiler_params=pltpu.CompilerParams(vmem_limit_bytes=60 * 1024 * 1024),
    )(*found)
    return site_level.reshape(-1), pixel_level.reshape(-1), duals.reshape(-1)


def solution(mesh):
    placed = (
        P("pix", None, "site"),
        P("pix", "site"),
        P("site"),
        P(),
        P("site"),
        P("pix"),
        P("site"),
        P("pix"),
        P("pix"),
    )
    return jax.shard_map(
        functools.partial(local, mesh.shape["pix"], mesh.shape["site"]),
        mesh=mesh,
        in_specs=placed,
        out_specs=(P("site"), P("pix"), P("pix")),
        check_vma=False,
    )
```

```python
import functools

import jax
import jax.numpy as jnp
from jax import lax
from jax.experimental import pallas as pl
from jax.experimental.pallas import tpu as pltpu
from jax.sharding import PartitionSpec as P

ITERS = 2
MARGIN_SCALE = 2.0 ** (-9)
LANES = 128
MESH = pl.DeviceIdType.MESH


def kernel(
    npix,
    nsite,
    margins_hbm,
    pos_hbm,
    ids_hbm,
    gain_hbm,
    price_hbm,
    weights_hbm,
    site_hbm,
    pixel_hbm,
    dual_hbm,
    site_hbm_out,
    pixel_hbm_out,
    dual_hbm_out,
    site_out,
    pixel_out,
    dual_out,
    margins_v,
    pos_ref,
    ids_ref,
    gain_ref,
    price_ref,
    weights_ref,
    site_ref,
    pixel_ref,
    dual_ref,
    tiles,
    tiles_t,
    dual_all,
    row_send,
    row_recv,
    col_recv,
    push_send,
    push_recv,
    tiles_recv,
    level_recv,
    margin_sem,
    small_sem,
    dual_sem,
    tile_sem,
    level_sem,
    row_sem,
    col_sem,
    push_sem,
):
    slots, width, sites = margins_v.shape
    cap = slots // npix
    halves = width // LANES
    rows = dual_ref.shape[0]
    me = lax.axis_index("pix")
    here = lax.axis_index("site")
    mine = here * npix + me

    def pix_peer(step):
        return lax.rem(me + step, npix)

    def site_peer(step):
        return lax.rem(here + step, nsite)

    far_first = sorted(range(nsite), key=lambda z: -min(z, nsite - z))
    peers = [(p, z) for z in far_first for p in range(npix) if p or z]

    small = [
        pltpu.make_async_copy(src, dst, small_sem.at[n])
        for n, (src, dst) in enumerate(
            (
                (dual_hbm, dual_ref),
                (pos_hbm, pos_ref),
                (ids_hbm, ids_ref),
                (gain_hbm, gain_ref),
                (price_hbm, price_ref),
                (weights_hbm, weights_ref),
                (site_hbm, site_ref),
                (pixel_hbm, pixel_ref),
            )
        )
    ]

    def margin_copy(t):
        part = pl.ds(t * cap, cap)
        return pltpu.make_async_copy(margins_hbm.at[part], margins_v.at[part], margin_sem.at[t])

    for copy in small:
        copy.start()
    for t in range(npix):
        margin_copy(t).start()

    barrier = pltpu.get_barrier_semaphore()
    for p, z in peers:
        pl.semaphore_signal(
            barrier, inc=1, device_id=(pix_peer(p), site_peer(z)), device_id_type=MESH
        )

    def send(src, dst, sems, p, z):
        pltpu.make_async_remote_copy(
            src_ref=src,
            dst_ref=dst,
            send_sem=sems.at[0],
            recv_sem=sems.at[1],
            device_id=(pix_peer(p), site_peer(z)),
            device_id_type=MESH,
        ).start()

    def drain(buffer, sem):
        part = buffer.at[pl.ds(0, buffer.shape[0] - 1)]
        pltpu.make_async_copy(part, part, sem).wait()

    for copy in small:
        copy.wait()
    dual_all[pl.ds(me, 1)] = dual_ref[...].astype(jnp.bfloat16)[None]

    diagonal = lax.broadcasted_iota(jnp.int32, (slots, slots), 0) == lax.broadcasted_iota(
        jnp.int32, (slots, slots), 1
    )
    pos = jnp.sum(
        jnp.where(diagonal, pos_ref[...].astype(jnp.float32), 0.0), axis=1, keepdims=True
    )
    slot_col = lax.broadcasted_iota(jnp.int32, (slots, 1), 0)
    first = ((slot_col // cap) * rows).astype(jnp.float32)
    base = jnp.where(pos >= 0.0, first + pos * halves, -1.0 * halves)
    row_id = lax.broadcasted_iota(jnp.int32, (slots, npix * rows), 1).astype(jnp.float32)
    choosers = [
        jnp.where(row_id == base + h, 1.0, 0.0).astype(jnp.bfloat16) for h in range(halves)
    ]
    pos_rows = jnp.broadcast_to(pos, (slots, LANES))
    for t in range(npix):
        row_send[t, halves * cap :, :] = pos_rows[t * cap : (t + 1) * cap]
    filled = jnp.broadcast_to(jnp.where(pos >= 0.0, 1.0, 0.0), (slots, width))
    slot_row = lax.broadcasted_iota(jnp.int32, (slots, width), 0) // cap
    slot_lane = lax.broadcasted_iota(jnp.int32, (slots, LANES), 0) % cap

    def of_target(t, values):
        return jnp.where(slot_row == t, values, 0.0).astype(jnp.bfloat16)

    def column_fold(sums):
        total = jnp.zeros((1, LANES), jnp.float32)
        for c in range(cap):
            part = sums[:, c * LANES : (c + 1) * LANES]
            total = total + jnp.sum(jnp.where(slot_lane == c, part, 0.0), axis=0, keepdims=True)
        return total

    lane_row = lax.broadcasted_iota(jnp.int32, (16, cap * LANES), 0)
    lane_cap = lax.broadcasted_iota(jnp.int32, (16, cap * LANES), 1) // LANES

    def spread_sites(values):
        wide = jnp.concatenate([values] * cap, axis=1)
        return jnp.where(lane_row == lane_cap, wide, 0.0).astype(jnp.bfloat16)

    chooser = (
        lax.broadcasted_iota(jnp.int32, (gain_ref.shape[0], sites), 0) == ids_ref[...]
    ).astype(jnp.float32)
    gain_half = 0.5 * lax.dot_general(
        gain_ref[...],
        chooser,
        (((0,), (0,)), ((), ())),
        precision=lax.Precision.HIGHEST,
        preferred_element_type=jnp.float32,
    )

    pl.semaphore_wait(barrier, len(peers))
    for p in range(1, npix):
        send(dual_all.at[me], dual_all.at[me], dual_sem, p, 0)

    def build(t):
        margin_copy(t).wait()
        for c in range(cap):
            part = slice(c * LANES, (c + 1) * LANES)
            values = margins_v[t * cap + c].astype(jnp.float32)
            values = 0.5 * jnp.tanh(values * (0.5 * MARGIN_SCALE) + gain_half) + 0.5
            values = values.astype(jnp.bfloat16)
            tiles[t, :, part] = values
            tiles_t[t, part, :] = values.T

    def build_and_send(step, carry):
        t = pix_peer(step)
        build(t)
        send(tiles.at[t], tiles_recv.at[me], tile_sem, step, 0)
        return carry

    lax.fori_loop(1, npix, build_and_send, 0)
    build(me)
    tiles_recv[pl.ds(me, 1)] = tiles[pl.ds(me, 1)]

    def fill_products(values, source):
        lhs = spread_sites(values)
        for t in range(npix):
            products = jnp.dot(lhs, tiles_t[t], preferred_element_type=jnp.float32)
            for h in range(halves):
                source[t, h * cap : (h + 1) * cap, :] = products[
                    :cap, h * LANES : (h + 1) * LANES
                ]

    def send_products(values, source, target, sems):
        fill_products(values, source)
        for p, z in peers:
            send(source.at[pix_peer(p)], target.at[mine], sems, p, z)
        target[pl.ds(mine, 1)] = source[pl.ds(me, 1)]

    state_row = lax.broadcasted_iota(jnp.int32, (rows, LANES), 0).astype(jnp.float32)

    def gather_group(z, buffer, first_line, total):
        for p in range(npix):
            s = z * npix + p
            for c in range(cap):
                line = row_recv[s, halves * cap + c : halves * cap + c + 1, :]
                offset = state_row - line * halves
                for h in range(halves):
                    line = buffer[first_line + p, h * cap + c : h * cap + c + 1, :]
                    total = total + jnp.where(offset == h, line, 0.0)
        return total

    no_rows = jnp.zeros((rows, LANES), jnp.float32)

    def gather_rows(buffer):
        def group(z, total):
            return gather_group(z, buffer, z * npix, total)

        return lax.fori_loop(0, nsite, group, no_rows)

    def column_totals(picked, groups, source):
        sums = jnp.zeros((len(groups) * slots, cap * LANES), jnp.float32)
        for t in range(npix):
            lhs = jnp.concatenate([of_target(t, group) for group in groups], axis=0)
            sums = sums + jnp.dot(lhs, source[t], preferred_element_type=jnp.float32)
        for n in range(len(groups)):
            total = column_fold(sums[n * slots : (n + 1) * slots])
            col_recv[picked, pl.ds(me, 1), n : n + 1] = total[None]
        for p in range(1, npix):
            send(col_recv.at[picked, me], col_recv.at[picked, me], col_sem.at[picked], p, 0)

    def pick(ch, values):
        return jnp.concatenate(
            [jnp.dot(c, values, preferred_element_type=jnp.float32) for c in ch], axis=1
        )

    site_level = site_ref[...]
    pixel_level = pixel_ref[...]
    duals = dual_ref[...]
    column_sum = None
    row_sum = None
    own_choosers = None
    for i in range(ITERS):
        if i == 0:
            drain(dual_all, dual_sem.at[1])
            selected = pick(choosers, dual_all[...].reshape(npix * rows, LANES))
            column_totals(i, [selected, filled], tiles)
        else:
            selected = pick(own_choosers, duals.astype(jnp.bfloat16))
            if i == 1:
                drain(tiles_recv, tile_sem.at[1])
            column_totals(i, [selected], tiles_recv)

        new_pixel = jnp.clip(pixel_level - (duals - weights_ref[...]), 0.0, 1.0)
        ahead = 2.0 * new_pixel - pixel_level
        if i == 0:
            send_products(jnp.ones((1, LANES), jnp.float32), row_send, row_recv, row_sem)
        if i == 1:
            for t in range(npix):
                tiles_t[t] = tiles_recv[t].T

        drain(col_recv.at[i], col_sem.at[i, 1])
        pulled = col_recv[i, 0]
        for s in range(1, npix):
            pulled = pulled + col_recv[i, s]
        if i == 0:
            column_sum = pulled[1:2]
        new_site = jnp.clip(site_level - (price_ref[...] - pulled[0:1] / column_sum), 0.0, 1.0)
        ahead_sites = 2.0 * new_site - site_level
        if i == 0:
            send_products(ahead_sites, push_send, push_recv, push_sem)
            drain(row_recv, row_sem.at[1])
            row_sum = gather_rows(row_recv) + 1.0
            arrived = jnp.concatenate(
                [
                    row_recv[here * npix + s, halves * cap : (halves + 1) * cap, :rows]
                    for s in range(npix)
                ],
                axis=0,
            )
            own_row = lax.broadcasted_iota(jnp.int32, (slots, rows), 1).astype(jnp.float32)
            own_choosers = [
                jnp.where(own_row == arrived * halves + h, 1.0, 0.0).astype(jnp.bfloat16)
                for h in range(halves)
            ]
            drain(push_recv, push_sem.at[1])
            pushed = gather_rows(push_recv)
        else:
            if i == 1:
                drain(push_recv, push_sem.at[0])
            fill_products(ahead_sites, push_send)
            level = level_recv.at[i - 1]
            level[pl.ds(here, 1)] = gather_group(here, push_send, 0, no_rows)[None]
            for z in far_first:
                if z:
                    send(level.at[here], level.at[here], level_sem.at[i - 1], 0, z)
            drain(level, level_sem.at[i - 1, 1])
            pushed = level[0]
            for z in range(1, nsite):
                pushed = pushed + level[z]
        duals = jnp.maximum(duals + (ahead - pushed) / row_sum, 0.0)
        site_level, pixel_level = new_site, new_pixel

    site_out[...] = site_level
    pixel_out[...] = pixel_level
    dual_out[...] = duals
    move_all(
        (site_out, pixel_out, dual_out),
        (site_hbm_out, pixel_hbm_out, dual_hbm_out),
        small_sem,
    )

    drain(row_recv, row_sem.at[0])
    drain(dual_all, dual_sem.at[0])
    drain(tiles_recv, tile_sem.at[0])
    for i in range(ITERS):
        drain(col_recv.at[i], col_sem.at[i, 0])
    for i in range(ITERS - 1):
        drain(level_recv.at[i], level_sem.at[i, 0])


def move_all(sources, targets, sem):
    copies = [
        pltpu.make_async_copy(src, dst, sem.at[n])
        for n, (src, dst) in enumerate(zip(sources, targets))
    ]
    for copy in copies:
        copy.start()
    for copy in copies:
        copy.wait()


def hand_on(site_in, pixel_in, dual_in, site_out, pixel_out, dual_out, site, pixel, dual, sem):
    held = (site, pixel, dual)
    move_all((site_in, pixel_in, dual_in), held, sem)
    move_all(held, (site_out, pixel_out, dual_out), sem)


def local(
    npix,
    nsite,
    margins,
    block_pos,
    pattern_ids,
    pattern_gain,
    site_price,
    weights,
    site_start,
    pixel_start,
    dual_start,
):
    slots, width, sites = margins.shape
    cap = slots // npix
    halves = width // LANES
    rows = weights.shape[0] // LANES
    devices = npix * nsite
    f32 = jnp.float32
    i32 = jnp.int32
    hbm = pl.BlockSpec(memory_space=pltpu.HBM)
    dma = pltpu.SemaphoreType.DMA
    results = (
        jax.ShapeDtypeStruct((1, sites), f32),
        jax.ShapeDtypeStruct((rows, LANES), f32),
        jax.ShapeDtypeStruct((rows, LANES), f32),
    )
    found = pl.pallas_call(
        functools.partial(kernel, npix, nsite),
        out_shape=results,
        in_specs=[hbm] * 9,
        out_specs=(hbm, hbm, hbm),
        scratch_shapes=[
            pltpu.VMEM((1, sites), f32),
            pltpu.VMEM((rows, LANES), f32),
            pltpu.VMEM((rows, LANES), f32),
            pltpu.VMEM((slots, width, sites), i32),
            pltpu.VMEM((1, slots), i32),
            pltpu.VMEM((1, sites), i32),
            pltpu.VMEM(pattern_gain.shape, f32),
            pltpu.VMEM((1, sites), f32),
            pltpu.VMEM((rows, LANES), f32),
            pltpu.VMEM((1, sites), f32),
            pltpu.VMEM((rows, LANES), f32),
            pltpu.VMEM((rows, LANES), f32),
            pltpu.VMEM((npix, width, cap * sites), jnp.bfloat16),
            pltpu.VMEM((npix, cap * sites, width), jnp.bfloat16),
            pltpu.VMEM((npix, rows, LANES), jnp.bfloat16),
            pltpu.VMEM((npix, (halves + 1) * cap, LANES), f32),
            pltpu.VMEM((devices, (halves + 1) * cap, LANES), f32),
            pltpu.VMEM((ITERS, npix, 2, LANES), f32),
            pltpu.VMEM((npix, halves * cap, LANES), f32),
            pltpu.VMEM((devices, halves * cap, LANES), f32),
            pltpu.VMEM((npix, width, cap * sites), jnp.bfloat16),
            pltpu.VMEM((ITERS - 1, nsite, rows, LANES), f32),
            dma((npix,)),
            dma((8,)),
            dma((2,)),
            dma((2,)),
            dma((ITERS - 1, 2)),
            dma((2,)),
            dma((ITERS, 2)),
            dma((2,)),
        ],
        compiler_params=pltpu.CompilerParams(
            collective_id=0, has_side_effects=True, vmem_limit_bytes=60 * 1024 * 1024
        ),
    )(
        margins,
        block_pos.reshape(1, slots),
        pattern_ids.reshape(1, sites),
        pattern_gain,
        site_price.reshape(1, sites),
        weights.reshape(rows, LANES),
        site_start.reshape(1, sites),
        pixel_start.reshape(rows, LANES),
        dual_start.reshape(rows, LANES),
    )
    site_level, pixel_level, duals = pl.pallas_call(
        hand_on,
        out_shape=results,
        in_specs=[hbm] * 3,
        out_specs=(hbm, hbm, hbm),
        scratch_shapes=[pltpu.VMEM(r.shape, f32) for r in results] + [dma((3,))],
        compiler_params=pltpu.CompilerParams(vmem_limit_bytes=60 * 1024 * 1024),
    )(*found)
    return site_level.reshape(-1), pixel_level.reshape(-1), duals.reshape(-1)


def solution(mesh):
    placed = (
        P("pix", None, "site"),
        P("pix", "site"),
        P("site"),
        P(),
        P("site"),
        P("pix"),
        P("site"),
        P("pix"),
        P("pix"),
    )
    return jax.shard_map(
        functools.partial(local, mesh.shape["pix"], mesh.shape["site"]),
        mesh=mesh,
        in_specs=placed,
        out_specs=(P("site"), P("pix"), P("pix")),
        check_vma=False,
    )
```

```python
import functools

import jax
import jax.numpy as jnp
from jax import lax
from jax.experimental import pallas as pl
from jax.experimental.pallas import tpu as pltpu
from jax.sharding import PartitionSpec as P

ITERS = 2
MARGIN_SCALE = 2.0 ** (-9)
LANES = 128
MESH = pl.DeviceIdType.MESH


def kernel(
    npix,
    nsite,
    margins_hbm,
    pos_hbm,
    ids_hbm,
    gain_hbm,
    price_hbm,
    weights_hbm,
    site_hbm,
    pixel_hbm,
    dual_hbm,
    site_hbm_out,
    pixel_hbm_out,
    dual_hbm_out,
    site_out,
    pixel_out,
    dual_out,
    margins_v,
    pos_ref,
    ids_ref,
    gain_ref,
    price_ref,
    weights_ref,
    site_ref,
    pixel_ref,
    dual_ref,
    tiles,
    tiles_t,
    dual_all,
    row_send,
    row_recv,
    col_recv,
    push_send,
    push_recv,
    margin_sem,
    small_sem,
    dual_sem,
    row_sem,
    col_sem,
    push_sem,
):
    slots, width, sites = margins_v.shape
    cap = slots // npix
    halves = width // LANES
    rows = dual_ref.shape[0]
    me = lax.axis_index("pix")
    here = lax.axis_index("site")
    mine = here * npix + me

    def pix_peer(step):
        return lax.rem(me + step, npix)

    def site_peer(step):
        return lax.rem(here + step, nsite)

    far_first = sorted(range(nsite), key=lambda z: -min(z, nsite - z))
    peers = [(p, z) for p in list(range(1, npix)) + [0] for z in far_first if p or z]

    small = [
        pltpu.make_async_copy(src, dst, small_sem.at[n])
        for n, (src, dst) in enumerate(
            (
                (dual_hbm, dual_ref),
                (pos_hbm, pos_ref),
                (ids_hbm, ids_ref),
                (gain_hbm, gain_ref),
                (price_hbm, price_ref),
                (weights_hbm, weights_ref),
                (site_hbm, site_ref),
                (pixel_hbm, pixel_ref),
            )
        )
    ]

    def margin_copy(t):
        part = pl.ds(t * cap, cap)
        return pltpu.make_async_copy(margins_hbm.at[part], margins_v.at[part], margin_sem.at[t])

    for copy in small:
        copy.start()
    for t in range(npix):
        margin_copy(t).start()

    barrier = pltpu.get_barrier_semaphore()
    for p, z in peers:
        pl.semaphore_signal(
            barrier, inc=1, device_id=(pix_peer(p), site_peer(z)), device_id_type=MESH
        )

    def send(src, dst, sems, p, z):
        pltpu.make_async_remote_copy(
            src_ref=src,
            dst_ref=dst,
            send_sem=sems.at[0],
            recv_sem=sems.at[1],
            device_id=(pix_peer(p), site_peer(z)),
            device_id_type=MESH,
        ).start()

    def drain(buffer, sem):
        part = buffer.at[pl.ds(0, buffer.shape[0] - 1)]
        pltpu.make_async_copy(part, part, sem).wait()

    def share_duals(i, values):
        dual_all[i, pl.ds(me, 1)] = values.astype(jnp.bfloat16)[None]

    def send_duals(i):
        for p in range(1, npix):
            send(dual_all.at[i, me], dual_all.at[i, me], dual_sem.at[i], p, 0)

    for copy in small:
        copy.wait()
    share_duals(0, dual_ref[...])

    diagonal = lax.broadcasted_iota(jnp.int32, (slots, slots), 0) == lax.broadcasted_iota(
        jnp.int32, (slots, slots), 1
    )
    pos = jnp.sum(
        jnp.where(diagonal, pos_ref[...].astype(jnp.float32), 0.0), axis=1, keepdims=True
    )
    slot_col = lax.broadcasted_iota(jnp.int32, (slots, 1), 0)
    first = ((slot_col // cap) * rows).astype(jnp.float32)
    base = jnp.where(pos >= 0.0, first + pos * halves, -1.0 * halves)
    row_id = lax.broadcasted_iota(jnp.int32, (slots, npix * rows), 1).astype(jnp.float32)
    choosers = [
        jnp.where(row_id == base + h, 1.0, 0.0).astype(jnp.bfloat16) for h in range(halves)
    ]
    pos_rows = jnp.broadcast_to(pos, (slots, LANES))
    for t in range(npix):
        row_send[t, halves * cap :, :] = pos_rows[t * cap : (t + 1) * cap]
    filled = jnp.broadcast_to(jnp.where(pos >= 0.0, 1.0, 0.0), (slots, width))
    slot_row = lax.broadcasted_iota(jnp.int32, (slots, width), 0) // cap
    slot_lane = lax.broadcasted_iota(jnp.int32, (slots, LANES), 0) % cap

    def of_target(t, values):
        return jnp.where(slot_row == t, values, 0.0).astype(jnp.bfloat16)

    def column_fold(sums):
        total = jnp.zeros((1, LANES), jnp.float32)
        for c in range(cap):
            part = sums[:, c * LANES : (c + 1) * LANES]
            total = total + jnp.sum(jnp.where(slot_lane == c, part, 0.0), axis=0, keepdims=True)
        return total

    lane_row = lax.broadcasted_iota(jnp.int32, (16, cap * LANES), 0)
    lane_cap = lax.broadcasted_iota(jnp.int32, (16, cap * LANES), 1) // LANES

    def spread_sites(values):
        wide = jnp.concatenate([values] * cap, axis=1)
        return jnp.where(lane_row == lane_cap, wide, 0.0).astype(jnp.bfloat16)

    chooser = (
        lax.broadcasted_iota(jnp.int32, (gain_ref.shape[0], sites), 0) == ids_ref[...]
    ).astype(jnp.float32)
    gain_half = 0.5 * lax.dot_general(
        gain_ref[...],
        chooser,
        (((0,), (0,)), ((), ())),
        precision=lax.Precision.HIGHEST,
        preferred_element_type=jnp.float32,
    )

    pl.semaphore_wait(barrier, len(peers))
    send_duals(0)

    def build(t, carry):
        margin_copy(t).wait()
        for c in range(cap):
            part = slice(c * LANES, (c + 1) * LANES)
            values = margins_v[t * cap + c].astype(jnp.float32)
            values = 0.5 * jnp.tanh(values * (0.5 * MARGIN_SCALE) + gain_half) + 0.5
            values = values.astype(jnp.bfloat16)
            tiles[t, :, part] = values
        return carry

    lax.fori_loop(0, npix, build, 0)

    def send_products(values, source, target, sems, turn):
        lhs = spread_sites(values)
        order = [pix_peer(p) for p in list(range(1, npix)) + [0]]

        def multiply(t):
            if turn:
                tiles_t[t] = tiles[t].T
            return jnp.dot(lhs, tiles_t[t], preferred_element_type=jnp.float32)

        ready = multiply(order[0])
        for n, t in enumerate(order):
            products = ready
            for h in range(halves):
                source[t, h * cap : (h + 1) * cap, :] = products[
                    :cap, h * LANES : (h + 1) * LANES
                ]
            if n + 1 < npix:
                ready = multiply(order[n + 1])
            p = (n + 1) % npix
            for z in far_first:
                if p or z:
                    send(source.at[t], target.at[mine], sems, p, z)
        target[pl.ds(mine, 1)] = source[pl.ds(me, 1)]

    state_row = lax.broadcasted_iota(jnp.int32, (rows, LANES), 0).astype(jnp.float32)

    def gather_rows(buffer):
        def group(z, total):
            for p in range(npix):
                s = z * npix + p
                for c in range(cap):
                    line = row_recv[s, halves * cap + c : halves * cap + c + 1, :]
                    offset = state_row - line * halves
                    for h in range(halves):
                        line = buffer[s, h * cap + c : h * cap + c + 1, :]
                        total = total + jnp.where(offset == h, line, 0.0)
            return total

        return lax.fori_loop(0, nsite, group, jnp.zeros((rows, LANES), jnp.float32))

    site_level = site_ref[...]
    pixel_level = pixel_ref[...]
    duals = dual_ref[...]
    column_sum = None
    row_sum = None
    for i in range(ITERS):
        drain(dual_all.at[i], dual_sem.at[i, 1])
        all_rows = dual_all[i].reshape(npix * rows, LANES)
        selected = jnp.concatenate(
            [jnp.dot(ch, all_rows, preferred_element_type=jnp.float32) for ch in choosers], axis=1
        )
        groups = [selected, filled] if i == 0 else [selected]
        sums = jnp.zeros((len(groups) * slots, cap * LANES), jnp.float32)
        for t in range(npix):
            lhs = jnp.concatenate([of_target(t, group) for group in groups], axis=0)
            sums = sums + jnp.dot(lhs, tiles[t], preferred_element_type=jnp.float32)
        for n in range(len(groups)):
            total = column_fold(sums[n * slots : (n + 1) * slots])
            col_recv[i, pl.ds(me, 1), n : n + 1] = total[None]
        for p in range(1, npix):
            send(col_recv.at[i, me], col_recv.at[i, me], col_sem.at[i], p, 0)

        new_pixel = jnp.clip(pixel_level - (duals - weights_ref[...]), 0.0, 1.0)
        ahead = 2.0 * new_pixel - pixel_level
        if i == 0:
            send_products(jnp.ones((1, LANES), jnp.float32), row_send, row_recv, row_sem, True)

        drain(col_recv.at[i], col_sem.at[i, 1])
        pulled = col_recv[i, 0]
        for s in range(1, npix):
            pulled = pulled + col_recv[i, s]
        if i == 0:
            column_sum = pulled[1:2]
        new_site = jnp.clip(site_level - (price_ref[...] - pulled[0:1] / column_sum), 0.0, 1.0)
        send_products(
            2.0 * new_site - site_level, push_send.at[i], push_recv.at[i], push_sem.at[i], False
        )
        if i == 0:
            drain(row_recv, row_sem.at[1])
            row_sum = gather_rows(row_recv) + 1.0
        drain(push_recv.at[i], push_sem.at[i, 1])
        pushed = gather_rows(push_recv.at[i])
        duals = jnp.maximum(duals + (ahead - pushed) / row_sum, 0.0)
        if i < ITERS - 1:
            share_duals(i + 1, duals)
            send_duals(i + 1)
        site_level, pixel_level = new_site, new_pixel

    site_out[...] = site_level
    pixel_out[...] = pixel_level
    dual_out[...] = duals
    move_all(
        (site_out, pixel_out, dual_out),
        (site_hbm_out, pixel_hbm_out, dual_hbm_out),
        small_sem,
    )

    drain(row_recv, row_sem.at[0])
    for i in range(ITERS):
        drain(dual_all.at[i], dual_sem.at[i, 0])
        drain(col_recv.at[i], col_sem.at[i, 0])
        drain(push_recv.at[i], push_sem.at[i, 0])


def move_all(sources, targets, sem):
    copies = [
        pltpu.make_async_copy(src, dst, sem.at[n])
        for n, (src, dst) in enumerate(zip(sources, targets))
    ]
    for copy in copies:
        copy.start()
    for copy in copies:
        copy.wait()


def hand_on(site_in, pixel_in, dual_in, site_out, pixel_out, dual_out, site, pixel, dual, sem):
    held = (site, pixel, dual)
    move_all((site_in, pixel_in, dual_in), held, sem)
    move_all(held, (site_out, pixel_out, dual_out), sem)


def local(
    npix,
    nsite,
    margins,
    block_pos,
    pattern_ids,
    pattern_gain,
    site_price,
    weights,
    site_start,
    pixel_start,
    dual_start,
):
    slots, width, sites = margins.shape
    cap = slots // npix
    halves = width // LANES
    rows = weights.shape[0] // LANES
    devices = npix * nsite
    f32 = jnp.float32
    i32 = jnp.int32
    hbm = pl.BlockSpec(memory_space=pltpu.HBM)
    dma = pltpu.SemaphoreType.DMA
    results = (
        jax.ShapeDtypeStruct((1, sites), f32),
        jax.ShapeDtypeStruct((rows, LANES), f32),
        jax.ShapeDtypeStruct((rows, LANES), f32),
    )
    found = pl.pallas_call(
        functools.partial(kernel, npix, nsite),
        out_shape=results,
        in_specs=[hbm] * 9,
        out_specs=(hbm, hbm, hbm),
        scratch_shapes=[
            pltpu.VMEM((1, sites), f32),
            pltpu.VMEM((rows, LANES), f32),
            pltpu.VMEM((rows, LANES), f32),
            pltpu.VMEM((slots, width, sites), i32),
            pltpu.VMEM((1, slots), i32),
            pltpu.VMEM((1, sites), i32),
            pltpu.VMEM(pattern_gain.shape, f32),
            pltpu.VMEM((1, sites), f32),
            pltpu.VMEM((rows, LANES), f32),
            pltpu.VMEM((1, sites), f32),
            pltpu.VMEM((rows, LANES), f32),
            pltpu.VMEM((rows, LANES), f32),
            pltpu.VMEM((npix, width, cap * sites), jnp.bfloat16),
            pltpu.VMEM((npix, cap * sites, width), jnp.bfloat16),
            pltpu.VMEM((ITERS, npix, rows, LANES), jnp.bfloat16),
            pltpu.VMEM((npix, (halves + 1) * cap, LANES), f32),
            pltpu.VMEM((devices, (halves + 1) * cap, LANES), f32),
            pltpu.VMEM((ITERS, npix, 2, LANES), f32),
            pltpu.VMEM((ITERS, npix, halves * cap, LANES), f32),
            pltpu.VMEM((ITERS, devices, halves * cap, LANES), f32),
            dma((npix,)),
            dma((8,)),
            dma((ITERS, 2)),
            dma((2,)),
            dma((ITERS, 2)),
            dma((ITERS, 2)),
        ],
        compiler_params=pltpu.CompilerParams(
            collective_id=0, has_side_effects=True, vmem_limit_bytes=60 * 1024 * 1024
        ),
    )(
        margins,
        block_pos.reshape(1, slots),
        pattern_ids.reshape(1, sites),
        pattern_gain,
        site_price.reshape(1, sites),
        weights.reshape(rows, LANES),
        site_start.reshape(1, sites),
        pixel_start.reshape(rows, LANES),
        dual_start.reshape(rows, LANES),
    )
    site_level, pixel_level, duals = pl.pallas_call(
        hand_on,
        out_shape=results,
        in_specs=[hbm] * 3,
        out_specs=(hbm, hbm, hbm),
        scratch_shapes=[pltpu.VMEM(r.shape, f32) for r in results] + [dma((3,))],
        compiler_params=pltpu.CompilerParams(vmem_limit_bytes=60 * 1024 * 1024),
    )(*found)
    return site_level.reshape(-1), pixel_level.reshape(-1), duals.reshape(-1)


def solution(mesh):
    placed = (
        P("pix", None, "site"),
        P("pix", "site"),
        P("site"),
        P(),
        P("site"),
        P("pix"),
        P("site"),
        P("pix"),
        P("pix"),
    )
    return jax.shard_map(
        functools.partial(local, mesh.shape["pix"], mesh.shape["site"]),
        mesh=mesh,
        in_specs=placed,
        out_specs=(P("site"), P("pix"), P("pix")),
        check_vma=False,
    )
```

```python
import functools

import jax
import jax.numpy as jnp
from jax import lax
from jax.experimental import pallas as pl
from jax.experimental.pallas import tpu as pltpu
from jax.sharding import PartitionSpec as P

ITERS = 2
MARGIN_SCALE = 2.0 ** (-9)
LANES = 128
MESH = pl.DeviceIdType.MESH


def kernel(
    npix,
    nsite,
    margins_hbm,
    pos_hbm,
    ids_hbm,
    gain_hbm,
    price_hbm,
    weights_hbm,
    site_hbm,
    pixel_hbm,
    dual_hbm,
    site_hbm_out,
    pixel_hbm_out,
    dual_hbm_out,
    site_out,
    pixel_out,
    dual_out,
    margins_v,
    pos_ref,
    ids_ref,
    gain_ref,
    price_ref,
    weights_ref,
    site_ref,
    pixel_ref,
    dual_ref,
    tiles,
    tiles_t,
    dual_all,
    row_send,
    row_recv,
    col_recv,
    push_send,
    push_recv,
    margin_sem,
    small_sem,
    dual_sem,
    row_sem,
    col_sem,
    push_sem,
):
    slots, width, sites = margins_v.shape
    cap = slots // npix
    halves = width // LANES
    rows = dual_ref.shape[0]
    me = lax.axis_index("pix")
    here = lax.axis_index("site")
    mine = here * npix + me

    def pix_peer(step):
        return lax.rem(me + step, npix)

    def site_peer(step):
        return lax.rem(here + step, nsite)

    far_first = sorted(range(nsite), key=lambda z: -min(z, nsite - z))

    small = [
        pltpu.make_async_copy(src, dst, small_sem.at[n])
        for n, (src, dst) in enumerate(
            (
                (dual_hbm, dual_ref),
                (pos_hbm, pos_ref),
                (ids_hbm, ids_ref),
                (gain_hbm, gain_ref),
                (price_hbm, price_ref),
                (weights_hbm, weights_ref),
                (site_hbm, site_ref),
                (pixel_hbm, pixel_ref),
            )
        )
    ]

    def margin_copy(t):
        part = pl.ds(t * cap, cap)
        return pltpu.make_async_copy(margins_hbm.at[part], margins_v.at[part], margin_sem.at[t])

    for copy in small:
        copy.start()
    @pl.loop(0, npix)
    def start_margins(t):
        margin_copy(t).start()

    barrier = pltpu.get_barrier_semaphore()

    def greet(p, z):
        pl.semaphore_signal(
            barrier, inc=1, device_id=(pix_peer(p), site_peer(z)), device_id_type=MESH
        )

    @pl.loop(1, npix)
    def greet_all(p):
        for z in far_first:
            greet(p, z)

    for z in far_first:
        if z:
            greet(0, z)

    def send(src, dst, sems, p, z):
        pltpu.make_async_remote_copy(
            src_ref=src,
            dst_ref=dst,
            send_sem=sems.at[0],
            recv_sem=sems.at[1],
            device_id=(pix_peer(p), site_peer(z)),
            device_id_type=MESH,
        ).start()

    def drain(buffer, sem):
        part = buffer.at[pl.ds(0, buffer.shape[0] - 1)]
        pltpu.make_async_copy(part, part, sem).wait()

    def share_duals(i, values):
        dual_all[i, pl.ds(me, 1)] = values.astype(jnp.bfloat16)[None]

    def send_duals(i):
        @pl.loop(1, npix)
        def send_all(p):
            send(dual_all.at[i, me], dual_all.at[i, me], dual_sem.at[i], p, 0)

    for copy in small:
        copy.wait()
    share_duals(0, dual_ref[...])

    diagonal = lax.broadcasted_iota(jnp.int32, (slots, slots), 0) == lax.broadcasted_iota(
        jnp.int32, (slots, slots), 1
    )
    pos = jnp.sum(
        jnp.where(diagonal, pos_ref[...].astype(jnp.float32), 0.0), axis=1, keepdims=True
    )
    slot_col = lax.broadcasted_iota(jnp.int32, (slots, 1), 0)
    first = ((slot_col // cap) * rows).astype(jnp.float32)
    base = jnp.where(pos >= 0.0, first + pos * halves, -1.0 * halves)
    row_id = lax.broadcasted_iota(jnp.int32, (slots, npix * rows), 1).astype(jnp.float32)
    choosers = [
        jnp.where(row_id == base + h, 1.0, 0.0).astype(jnp.bfloat16) for h in range(halves)
    ]
    pos_rows = jnp.broadcast_to(pos, (slots, LANES))
    for t in range(npix):
        row_send[t, halves * cap :, :] = pos_rows[t * cap : (t + 1) * cap]
    filled = jnp.broadcast_to(jnp.where(pos >= 0.0, 1.0, 0.0), (slots, width))
    slot_row = lax.broadcasted_iota(jnp.int32, (slots, width), 0) // cap
    slot_lane = lax.broadcasted_iota(jnp.int32, (slots, LANES), 0) % cap

    def of_target(t, values):
        return jnp.where(slot_row == t, values, 0.0).astype(jnp.bfloat16)

    def column_fold(sums):
        total = jnp.zeros((1, LANES), jnp.float32)
        for c in range(cap):
            part = sums[:, c * LANES : (c + 1) * LANES]
            total = total + jnp.sum(jnp.where(slot_lane == c, part, 0.0), axis=0, keepdims=True)
        return total

    lane_row = lax.broadcasted_iota(jnp.int32, (16, cap * LANES), 0)
    lane_cap = lax.broadcasted_iota(jnp.int32, (16, cap * LANES), 1) // LANES

    def spread_sites(values):
        wide = jnp.concatenate([values] * cap, axis=1)
        return jnp.where(lane_row == lane_cap, wide, 0.0).astype(jnp.bfloat16)

    chooser = (
        lax.broadcasted_iota(jnp.int32, (gain_ref.shape[0], sites), 0) == ids_ref[...]
    ).astype(jnp.float32)
    gain_half = 0.5 * lax.dot_general(
        gain_ref[...],
        chooser,
        (((0,), (0,)), ((), ())),
        precision=lax.Precision.HIGHEST,
        preferred_element_type=jnp.float32,
    )

    pl.semaphore_wait(barrier, npix * nsite - 1)
    send_duals(0)

    def build(t, carry):
        margin_copy(t).wait()
        for c in range(cap):
            part = slice(c * LANES, (c + 1) * LANES)
            values = margins_v[t * cap + c].astype(jnp.float32)
            values = 0.5 * jnp.tanh(values * (0.5 * MARGIN_SCALE) + gain_half) + 0.5
            values = values.astype(jnp.bfloat16)
            tiles[t, :, part] = values
        return carry

    lax.fori_loop(0, npix, build, 0)

    def send_products(values, source, target, sems, turn):
        lhs = spread_sites(values)

        def multiply(t):
            if turn:
                tiles_t[t] = tiles[t].T
            return jnp.dot(lhs, tiles_t[t], preferred_element_type=jnp.float32)

        def put(t, products):
            for h in range(halves):
                source[t, h * cap : (h + 1) * cap, :] = products[
                    :cap, h * LANES : (h + 1) * LANES
                ]

        def go(p, ready):
            t = pix_peer(p)
            put(t, ready)
            following = multiply(pix_peer(p + 1))
            for z in far_first:
                send(source.at[t], target.at[mine], sems, p, z)
            return following

        put(me, lax.fori_loop(1, npix, go, multiply(pix_peer(1))))
        for z in far_first:
            if z:
                send(source.at[me], target.at[mine], sems, 0, z)
        target[pl.ds(mine, 1)] = source[pl.ds(me, 1)]

    state_row = lax.broadcasted_iota(jnp.int32, (rows, LANES), 0).astype(jnp.float32)

    def gather_rows(buffer):
        def group(z, total):
            for p in range(npix):
                s = z * npix + p
                for c in range(cap):
                    line = row_recv[s, halves * cap + c : halves * cap + c + 1, :]
                    offset = state_row - line * halves
                    for h in range(halves):
                        line = buffer[s, h * cap + c : h * cap + c + 1, :]
                        total = total + jnp.where(offset == h, line, 0.0)
            return total

        return lax.fori_loop(0, nsite, group, jnp.zeros((rows, LANES), jnp.float32))

    site_level = site_ref[...]
    pixel_level = pixel_ref[...]
    duals = dual_ref[...]
    column_sum = None
    row_sum = None
    for i in range(ITERS):
        drain(dual_all.at[i], dual_sem.at[i, 1])
        all_rows = dual_all[i].reshape(npix * rows, LANES)
        selected = jnp.concatenate(
            [jnp.dot(ch, all_rows, preferred_element_type=jnp.float32) for ch in choosers], axis=1
        )
        groups = [selected, filled] if i == 0 else [selected]
        sums = jnp.zeros((len(groups) * slots, cap * LANES), jnp.float32)
        for t in range(npix):
            lhs = jnp.concatenate([of_target(t, group) for group in groups], axis=0)
            sums = sums + jnp.dot(lhs, tiles[t], preferred_element_type=jnp.float32)
        for n in range(len(groups)):
            total = column_fold(sums[n * slots : (n + 1) * slots])
            col_recv[i, pl.ds(me, 1), n : n + 1] = total[None]
        @pl.loop(1, npix)
        def send_columns(p):
            send(col_recv.at[i, me], col_recv.at[i, me], col_sem.at[i], p, 0)

        new_pixel = jnp.clip(pixel_level - (duals - weights_ref[...]), 0.0, 1.0)
        ahead = 2.0 * new_pixel - pixel_level
        if i == 0:
            send_products(jnp.ones((1, LANES), jnp.float32), row_send, row_recv, row_sem, True)

        drain(col_recv.at[i], col_sem.at[i, 1])
        pulled = col_recv[i, 0]
        for s in range(1, npix):
            pulled = pulled + col_recv[i, s]
        if i == 0:
            column_sum = pulled[1:2]
        new_site = jnp.clip(site_level - (price_ref[...] - pulled[0:1] / column_sum), 0.0, 1.0)
        send_products(
            2.0 * new_site - site_level, push_send.at[i], push_recv.at[i], push_sem.at[i], False
        )
        if i == 0:
            drain(row_recv, row_sem.at[1])
            row_sum = gather_rows(row_recv) + 1.0
        drain(push_recv.at[i], push_sem.at[i, 1])
        pushed = gather_rows(push_recv.at[i])
        duals = jnp.maximum(duals + (ahead - pushed) / row_sum, 0.0)
        if i < ITERS - 1:
            share_duals(i + 1, duals)
            send_duals(i + 1)
        site_level, pixel_level = new_site, new_pixel

    site_out[...] = site_level
    pixel_out[...] = pixel_level
    dual_out[...] = duals
    move_all(
        (site_out, pixel_out, dual_out),
        (site_hbm_out, pixel_hbm_out, dual_hbm_out),
        small_sem,
    )

    drain(row_recv, row_sem.at[0])
    for i in range(ITERS):
        drain(dual_all.at[i], dual_sem.at[i, 0])
        drain(col_recv.at[i], col_sem.at[i, 0])
        drain(push_recv.at[i], push_sem.at[i, 0])


def move_all(sources, targets, sem):
    copies = [
        pltpu.make_async_copy(src, dst, sem.at[n])
        for n, (src, dst) in enumerate(zip(sources, targets))
    ]
    for copy in copies:
        copy.start()
    for copy in copies:
        copy.wait()


def hand_on(site_in, pixel_in, dual_in, site_out, pixel_out, dual_out, site, pixel, dual, sem):
    held = (site, pixel, dual)
    move_all((site_in, pixel_in, dual_in), held, sem)
    move_all(held, (site_out, pixel_out, dual_out), sem)


def local(
    npix,
    nsite,
    margins,
    block_pos,
    pattern_ids,
    pattern_gain,
    site_price,
    weights,
    site_start,
    pixel_start,
    dual_start,
):
    slots, width, sites = margins.shape
    cap = slots // npix
    halves = width // LANES
    rows = weights.shape[0] // LANES
    devices = npix * nsite
    f32 = jnp.float32
    i32 = jnp.int32
    hbm = pl.BlockSpec(memory_space=pltpu.HBM)
    dma = pltpu.SemaphoreType.DMA
    results = (
        jax.ShapeDtypeStruct((1, sites), f32),
        jax.ShapeDtypeStruct((rows, LANES), f32),
        jax.ShapeDtypeStruct((rows, LANES), f32),
    )
    found = pl.pallas_call(
        functools.partial(kernel, npix, nsite),
        out_shape=results,
        in_specs=[hbm] * 9,
        out_specs=(hbm, hbm, hbm),
        scratch_shapes=[
            pltpu.VMEM((1, sites), f32),
            pltpu.VMEM((rows, LANES), f32),
            pltpu.VMEM((rows, LANES), f32),
            pltpu.VMEM((slots, width, sites), i32),
            pltpu.VMEM((1, slots), i32),
            pltpu.VMEM((1, sites), i32),
            pltpu.VMEM(pattern_gain.shape, f32),
            pltpu.VMEM((1, sites), f32),
            pltpu.VMEM((rows, LANES), f32),
            pltpu.VMEM((1, sites), f32),
            pltpu.VMEM((rows, LANES), f32),
            pltpu.VMEM((rows, LANES), f32),
            pltpu.VMEM((npix, width, cap * sites), jnp.bfloat16),
            pltpu.VMEM((npix, cap * sites, width), jnp.bfloat16),
            pltpu.VMEM((ITERS, npix, rows, LANES), jnp.bfloat16),
            pltpu.VMEM((npix, (halves + 1) * cap, LANES), f32),
            pltpu.VMEM((devices, (halves + 1) * cap, LANES), f32),
            pltpu.VMEM((ITERS, npix, 2, LANES), f32),
            pltpu.VMEM((ITERS, npix, halves * cap, LANES), f32),
            pltpu.VMEM((ITERS, devices, halves * cap, LANES), f32),
            dma((npix,)),
            dma((8,)),
            dma((ITERS, 2)),
            dma((2,)),
            dma((ITERS, 2)),
            dma((ITERS, 2)),
        ],
        compiler_params=pltpu.CompilerParams(
            collective_id=0, has_side_effects=True, vmem_limit_bytes=60 * 1024 * 1024
        ),
    )(
        margins,
        block_pos.reshape(1, slots),
        pattern_ids.reshape(1, sites),
        pattern_gain,
        site_price.reshape(1, sites),
        weights.reshape(rows, LANES),
        site_start.reshape(1, sites),
        pixel_start.reshape(rows, LANES),
        dual_start.reshape(rows, LANES),
    )
    site_level, pixel_level, duals = pl.pallas_call(
        hand_on,
        out_shape=results,
        in_specs=[hbm] * 3,
        out_specs=(hbm, hbm, hbm),
        scratch_shapes=[pltpu.VMEM(r.shape, f32) for r in results] + [dma((3,))],
        compiler_params=pltpu.CompilerParams(vmem_limit_bytes=60 * 1024 * 1024),
    )(*found)
    return site_level.reshape(-1), pixel_level.reshape(-1), duals.reshape(-1)


def solution(mesh):
    placed = (
        P("pix", None, "site"),
        P("pix", "site"),
        P("site"),
        P(),
        P("site"),
        P("pix"),
        P("site"),
        P("pix"),
        P("pix"),
    )
    return jax.shard_map(
        functools.partial(local, mesh.shape["pix"], mesh.shape["site"]),
        mesh=mesh,
        in_specs=placed,
        out_specs=(P("site"), P("pix"), P("pix")),
        check_vma=False,
    )
```

```python
import functools

import jax
import jax.numpy as jnp
from jax import lax
from jax.experimental import pallas as pl
from jax.experimental.pallas import tpu as pltpu
from jax.sharding import PartitionSpec as P

ITERS = 2
MARGIN_SCALE = 2.0 ** (-9)
LANES = 128
MESH = pl.DeviceIdType.MESH


def kernel(
    npix,
    nsite,
    margins_hbm,
    pos_hbm,
    ids_hbm,
    gain_hbm,
    price_hbm,
    weights_hbm,
    site_hbm,
    pixel_hbm,
    dual_hbm,
    site_hbm_out,
    pixel_hbm_out,
    dual_hbm_out,
    site_out,
    pixel_out,
    dual_out,
    margins_v,
    pos_ref,
    ids_ref,
    gain_ref,
    price_ref,
    weights_ref,
    site_ref,
    pixel_ref,
    dual_ref,
    tiles,
    tiles_t,
    dual_all,
    row_send,
    row_recv,
    col_recv,
    push_send,
    push_recv,
    parts,
    margin_sem,
    small_sem,
    dual_sem,
    row_sem,
    col_sem,
    push_sem,
):
    slots, width, sites = margins_v.shape
    cap = slots // npix
    halves = width // LANES
    rows = dual_ref.shape[0]
    me = lax.axis_index("pix")
    here = lax.axis_index("site")
    mine = here * npix + me

    pix_ids = [me] + [lax.rem(me + step, npix) for step in range(1, npix)]
    site_ids = [here] + [lax.rem(here + step, nsite) for step in range(1, nsite)]

    def pix_peer(step):
        return pix_ids[step]

    def site_peer(step):
        return site_ids[step]

    far_first = sorted(range(nsite), key=lambda z: -min(z, nsite - z))
    peers = [(p, z) for p in list(range(1, npix)) + [0] for z in far_first if p or z]

    small = [
        pltpu.make_async_copy(src, dst, small_sem.at[n])
        for n, (src, dst) in enumerate(
            (
                (dual_hbm, dual_ref),
                (pos_hbm, pos_ref),
                (ids_hbm, ids_ref),
                (gain_hbm, gain_ref),
                (price_hbm, price_ref),
                (weights_hbm, weights_ref),
                (site_hbm, site_ref),
                (pixel_hbm, pixel_ref),
            )
        )
    ]

    def margin_copy(t):
        part = pl.ds(t * cap, cap)
        return pltpu.make_async_copy(margins_hbm.at[part], margins_v.at[part], margin_sem.at[t])

    barrier = pltpu.get_barrier_semaphore()
    for p, z in peers:
        pl.semaphore_signal(
            barrier, inc=1, device_id=(pix_peer(p), site_peer(z)), device_id_type=MESH
        )

    for copy in small:
        copy.start()
    for t in range(npix):
        margin_copy(t).start()

    def send(src, dst, sems, p, z):
        pltpu.make_async_remote_copy(
            src_ref=src,
            dst_ref=dst,
            send_sem=sems.at[0],
            recv_sem=sems.at[1],
            device_id=(pix_peer(p), site_peer(z)),
            device_id_type=MESH,
        ).start()

    def drain(buffer, sem):
        part = buffer.at[pl.ds(0, buffer.shape[0] - 1)]
        pltpu.make_async_copy(part, part, sem).wait()

    def share_duals(i, values):
        dual_all[i, pl.ds(me, 1)] = values.astype(jnp.bfloat16)[None]

    def send_duals(i):
        for p in range(1, npix):
            send(dual_all.at[i, me], dual_all.at[i, me], dual_sem.at[i], p, 0)

    for copy in small:
        copy.wait()
    share_duals(0, dual_ref[...])

    diagonal = lax.broadcasted_iota(jnp.int32, (slots, slots), 0) == lax.broadcasted_iota(
        jnp.int32, (slots, slots), 1
    )
    pos = jnp.sum(
        jnp.where(diagonal, pos_ref[...].astype(jnp.float32), 0.0), axis=1, keepdims=True
    )
    slot_col = lax.broadcasted_iota(jnp.int32, (slots, 1), 0)
    first = ((slot_col // cap) * rows).astype(jnp.float32)
    base = jnp.where(pos >= 0.0, first + pos * halves, -1.0 * halves)
    row_id = lax.broadcasted_iota(jnp.int32, (slots, npix * rows), 1).astype(jnp.float32)
    choosers = [
        jnp.where(row_id == base + h, 1.0, 0.0).astype(jnp.bfloat16) for h in range(halves)
    ]
    pos_rows = jnp.broadcast_to(pos, (slots, LANES))
    for t in range(npix):
        row_send[t, halves * cap :, :] = pos_rows[t * cap : (t + 1) * cap]
    filled = jnp.broadcast_to(jnp.where(pos >= 0.0, 1.0, 0.0), (slots, width))
    slot_row = lax.broadcasted_iota(jnp.int32, (slots, width), 0) // cap
    slot_lane = lax.broadcasted_iota(jnp.int32, (slots, LANES), 0) % cap

    def of_target(t, values):
        return jnp.where(slot_row == t, values, 0.0).astype(jnp.bfloat16)

    def column_fold(sums):
        total = jnp.zeros((1, LANES), jnp.float32)
        for c in range(cap):
            part = sums[:, c * LANES : (c + 1) * LANES]
            total = total + jnp.sum(jnp.where(slot_lane == c, part, 0.0), axis=0, keepdims=True)
        return total

    lane_row = lax.broadcasted_iota(jnp.int32, (16, cap * LANES), 0)
    lane_cap = lax.broadcasted_iota(jnp.int32, (16, cap * LANES), 1) // LANES

    def spread_sites(values):
        wide = jnp.concatenate([values] * cap, axis=1)
        return jnp.where(lane_row == lane_cap, wide, 0.0).astype(jnp.bfloat16)

    chooser = (
        lax.broadcasted_iota(jnp.int32, (gain_ref.shape[0], sites), 0) == ids_ref[...]
    ).astype(jnp.float32)
    gain_half = 0.5 * lax.dot_general(
        gain_ref[...],
        chooser,
        (((0,), (0,)), ((), ())),
        precision=lax.Precision.HIGHEST,
        preferred_element_type=jnp.float32,
    )

    pl.semaphore_wait(barrier, len(peers))
    send_duals(0)

    def build(t, carry):
        margin_copy(t).wait()
        for c in range(cap):
            part = slice(c * LANES, (c + 1) * LANES)
            values = margins_v[t * cap + c].astype(jnp.float32)
            values = 0.5 * jnp.tanh(values * (0.5 * MARGIN_SCALE) + gain_half) + 0.5
            values = values.astype(jnp.bfloat16)
            tiles[t, :, part] = values
        return carry

    lax.fori_loop(0, npix, build, 0)

    order = list(range(1, npix)) + [0]

    def multiply(lhs, t):
        return jnp.dot(lhs, tiles_t[t], preferred_element_type=jnp.float32)

    def put(target, t, products):
        for h in range(halves):
            target[t, h * cap : (h + 1) * cap, :] = products[:cap, h * LANES : (h + 1) * LANES]

    def send_lines(source, target, sems, arrival, p):
        t = pix_peer(p)
        for z in far_first:
            if p or z:
                pltpu.make_async_remote_copy(
                    src_ref=source.at[t],
                    dst_ref=target.at[mine],
                    send_sem=sems.at[0],
                    recv_sem=arrival,
                    device_id=(t, site_peer(z)),
                    device_id_type=MESH,
                ).start()

    def send_products(values, source, target, sems):
        lhs = spread_sites(values)
        ready = multiply(lhs, pix_peer(order[0]))
        for n, p in enumerate(order):
            put(source, pix_peer(p), ready)
            if n + 1 < npix:
                ready = multiply(lhs, pix_peer(order[n + 1]))
            send_lines(source, target, sems, sems.at[1 + here], p)
        target[pl.ds(mine, 1)] = source[pl.ds(me, 1)]

    lhs = spread_sites(jnp.ones((1, LANES), jnp.float32))
    for t in range(npix):
        tiles_t[t] = tiles[t].T
        put(row_send, t, multiply(lhs, t))

    state_row = lax.broadcasted_iota(jnp.int32, (rows, LANES), 0).astype(jnp.float32)

    def gather_group(z, buffer):
        total = jnp.zeros((rows, LANES), jnp.float32)
        for p in range(npix):
            s = z * npix + p
            for c in range(cap):
                line = row_recv[s, halves * cap + c : halves * cap + c + 1, :]
                offset = state_row - line * halves
                for h in range(halves):
                    line = buffer[s, h * cap + c : h * cap + c + 1, :]
                    total = total + jnp.where(offset == h, line, 0.0)
        parts[z] = total

    def gather_rows(buffer, arrivals):
        def wait_for(z, count):
            if arrivals is not None:
                part = buffer.at[pl.ds(z * npix, count)]
                pltpu.make_async_copy(part, part, arrivals.at[1 + z]).wait()

        wait_for(here, npix - 1)
        gather_group(here, buffer)

        @pl.loop(1, nsite)
        def others(step):
            z = lax.rem(here + step, nsite)
            wait_for(z, npix)
            gather_group(z, buffer)

        total = parts[0]
        for z in range(1, nsite):
            total = total + parts[z]
        return total

    site_level = site_ref[...]
    pixel_level = pixel_ref[...]
    duals = dual_ref[...]
    column_sum = None
    row_sum = None
    for i in range(ITERS):
        drain(dual_all.at[i], dual_sem.at[i, 1])
        all_rows = dual_all[i].reshape(npix * rows, LANES)
        selected = jnp.concatenate(
            [jnp.dot(ch, all_rows, preferred_element_type=jnp.float32) for ch in choosers], axis=1
        )
        groups = [selected, filled] if i == 0 else [selected]
        sums = jnp.zeros((len(groups) * slots, cap * LANES), jnp.float32)
        for t in range(npix):
            lhs = jnp.concatenate([of_target(t, group) for group in groups], axis=0)
            sums = sums + jnp.dot(lhs, tiles[t], preferred_element_type=jnp.float32)
        for n in range(len(groups)):
            total = column_fold(sums[n * slots : (n + 1) * slots])
            col_recv[i, pl.ds(me, 1), n : n + 1] = total[None]
        for p in range(1, npix):
            send(col_recv.at[i, me], col_recv.at[i, me], col_sem.at[i], p, 0)

        new_pixel = jnp.clip(pixel_level - (duals - weights_ref[...]), 0.0, 1.0)
        ahead = 2.0 * new_pixel - pixel_level
        if i == 0:
            for p in order:
                send_lines(row_send, row_recv, row_sem, row_sem.at[1], p)
            row_recv[pl.ds(mine, 1)] = row_send[pl.ds(me, 1)]

        drain(col_recv.at[i], col_sem.at[i, 1])
        pulled = col_recv[i, 0]
        for s in range(1, npix):
            pulled = pulled + col_recv[i, s]
        if i == 0:
            column_sum = pulled[1:2]
        new_site = jnp.clip(site_level - (price_ref[...] - pulled[0:1] / column_sum), 0.0, 1.0)
        send_products(
            2.0 * new_site - site_level, push_send.at[i], push_recv.at[i], push_sem.at[i]
        )
        if i == 0:
            drain(row_recv, row_sem.at[1])
            row_sum = gather_rows(row_recv, None) + 1.0
        pushed = gather_rows(push_recv.at[i], push_sem.at[i])
        duals = jnp.maximum(duals + (ahead - pushed) / row_sum, 0.0)
        if i < ITERS - 1:
            share_duals(i + 1, duals)
            send_duals(i + 1)
        site_level, pixel_level = new_site, new_pixel

    site_out[...] = site_level
    pixel_out[...] = pixel_level
    dual_out[...] = duals
    move_all(
        (site_out, pixel_out, dual_out),
        (site_hbm_out, pixel_hbm_out, dual_hbm_out),
        small_sem,
    )

    drain(row_recv, row_sem.at[0])
    for i in range(ITERS):
        drain(dual_all.at[i], dual_sem.at[i, 0])
        drain(col_recv.at[i], col_sem.at[i, 0])
        drain(push_recv.at[i], push_sem.at[i, 0])


def move_all(sources, targets, sem):
    copies = [
        pltpu.make_async_copy(src, dst, sem.at[n])
        for n, (src, dst) in enumerate(zip(sources, targets))
    ]
    for copy in copies:
        copy.start()
    for copy in copies:
        copy.wait()


def hand_on(site_in, pixel_in, dual_in, site_out, pixel_out, dual_out, site, pixel, dual, sem):
    held = (site, pixel, dual)
    move_all((site_in, pixel_in, dual_in), held, sem)
    move_all(held, (site_out, pixel_out, dual_out), sem)


def local(
    npix,
    nsite,
    margins,
    block_pos,
    pattern_ids,
    pattern_gain,
    site_price,
    weights,
    site_start,
    pixel_start,
    dual_start,
):
    slots, width, sites = margins.shape
    cap = slots // npix
    halves = width // LANES
    rows = weights.shape[0] // LANES
    devices = npix * nsite
    f32 = jnp.float32
    i32 = jnp.int32
    hbm = pl.BlockSpec(memory_space=pltpu.HBM)
    dma = pltpu.SemaphoreType.DMA
    results = (
        jax.ShapeDtypeStruct((1, sites), f32),
        jax.ShapeDtypeStruct((rows, LANES), f32),
        jax.ShapeDtypeStruct((rows, LANES), f32),
    )
    found = pl.pallas_call(
        functools.partial(kernel, npix, nsite),
        out_shape=results,
        in_specs=[hbm] * 9,
        out_specs=(hbm, hbm, hbm),
        scratch_shapes=[
            pltpu.VMEM((1, sites), f32),
            pltpu.VMEM((rows, LANES), f32),
            pltpu.VMEM((rows, LANES), f32),
            pltpu.VMEM((slots, width, sites), i32),
            pltpu.VMEM((1, slots), i32),
            pltpu.VMEM((1, sites), i32),
            pltpu.VMEM(pattern_gain.shape, f32),
            pltpu.VMEM((1, sites), f32),
            pltpu.VMEM((rows, LANES), f32),
            pltpu.VMEM((1, sites), f32),
            pltpu.VMEM((rows, LANES), f32),
            pltpu.VMEM((rows, LANES), f32),
            pltpu.VMEM((npix, width, cap * sites), jnp.bfloat16),
            pltpu.VMEM((npix, cap * sites, width), jnp.bfloat16),
            pltpu.VMEM((ITERS, npix, rows, LANES), jnp.bfloat16),
            pltpu.VMEM((npix, (halves + 1) * cap, LANES), f32),
            pltpu.VMEM((devices, (halves + 1) * cap, LANES), f32),
            pltpu.VMEM((ITERS, npix, 2, LANES), f32),
            pltpu.VMEM((ITERS, npix, halves * cap, LANES), f32),
            pltpu.VMEM((ITERS, devices, halves * cap, LANES), f32),
            pltpu.VMEM((nsite, rows, LANES), f32),
            dma((npix,)),
            dma((8,)),
            dma((ITERS, 2)),
            dma((2,)),
            dma((ITERS, 2)),
            dma((ITERS, 1 + nsite)),
        ],
        compiler_params=pltpu.CompilerParams(
            collective_id=0, has_side_effects=True, vmem_limit_bytes=60 * 1024 * 1024
        ),
    )(
        margins,
        block_pos.reshape(1, slots),
        pattern_ids.reshape(1, sites),
        pattern_gain,
        site_price.reshape(1, sites),
        weights.reshape(rows, LANES),
        site_start.reshape(1, sites),
        pixel_start.reshape(rows, LANES),
        dual_start.reshape(rows, LANES),
    )
    site_level, pixel_level, duals = pl.pallas_call(
        hand_on,
        out_shape=results,
        in_specs=[hbm] * 3,
        out_specs=(hbm, hbm, hbm),
        scratch_shapes=[pltpu.VMEM(r.shape, f32) for r in results] + [dma((3,))],
        compiler_params=pltpu.CompilerParams(vmem_limit_bytes=60 * 1024 * 1024),
    )(*found)
    return site_level.reshape(-1), pixel_level.reshape(-1), duals.reshape(-1)


def solution(mesh):
    placed = (
        P("pix", None, "site"),
        P("pix", "site"),
        P("site"),
        P(),
        P("site"),
        P("pix"),
        P("site"),
        P("pix"),
        P("pix"),
    )
    return jax.shard_map(
        functools.partial(local, mesh.shape["pix"], mesh.shape["site"]),
        mesh=mesh,
        in_specs=placed,
        out_specs=(P("site"), P("pix"), P("pix")),
        check_vma=False,
    )
```

```python
import functools

import jax
import jax.numpy as jnp
from jax import lax
from jax.experimental import pallas as pl
from jax.experimental.pallas import tpu as pltpu
from jax.sharding import PartitionSpec as P

ITERS = 2
MARGIN_SCALE = 2.0 ** (-9)
LANES = 128
MESH = pl.DeviceIdType.MESH


def kernel(
    npix,
    nsite,
    margins_hbm,
    pos_hbm,
    ids_hbm,
    gain_hbm,
    price_hbm,
    weights_hbm,
    site_hbm,
    pixel_hbm,
    dual_hbm,
    site_hbm_out,
    pixel_hbm_out,
    dual_hbm_out,
    site_out,
    pixel_out,
    dual_out,
    margins_v,
    pos_ref,
    ids_ref,
    gain_ref,
    price_ref,
    weights_ref,
    site_ref,
    pixel_ref,
    dual_ref,
    tiles,
    tiles_t,
    dual_all,
    row_send,
    row_recv,
    col_recv,
    push_send,
    push_recv,
    parts,
    level_recv,
    level_sem,
    margin_sem,
    small_sem,
    dual_sem,
    row_sem,
    col_sem,
    push_sem,
):
    slots, width, sites = margins_v.shape
    cap = slots // npix
    halves = width // LANES
    rows = dual_ref.shape[0]
    me = lax.axis_index("pix")
    here = lax.axis_index("site")
    mine = here * npix + me

    pix_ids = [me] + [lax.rem(me + step, npix) for step in range(1, npix)]
    site_ids = [here] + [lax.rem(here + step, nsite) for step in range(1, nsite)]

    def pix_peer(step):
        return pix_ids[step]

    def site_peer(step):
        return site_ids[step]

    far_first = sorted(range(nsite), key=lambda z: -min(z, nsite - z))
    peers = [(p, z) for p in list(range(1, npix)) + [0] for z in far_first if p or z]

    small = [
        pltpu.make_async_copy(src, dst, small_sem.at[n])
        for n, (src, dst) in enumerate(
            (
                (dual_hbm, dual_ref),
                (pos_hbm, pos_ref),
                (ids_hbm, ids_ref),
                (gain_hbm, gain_ref),
                (price_hbm, price_ref),
                (weights_hbm, weights_ref),
                (site_hbm, site_ref),
                (pixel_hbm, pixel_ref),
            )
        )
    ]

    def margin_copy(t):
        part = pl.ds(t * cap, cap)
        return pltpu.make_async_copy(margins_hbm.at[part], margins_v.at[part], margin_sem.at[t])

    barrier = pltpu.get_barrier_semaphore()
    for p, z in peers:
        pl.semaphore_signal(
            barrier, inc=1, device_id=(pix_peer(p), site_peer(z)), device_id_type=MESH
        )

    for copy in small:
        copy.start()
    for t in range(npix):
        margin_copy(t).start()

    def send(src, dst, sems, p, z):
        pltpu.make_async_remote_copy(
            src_ref=src,
            dst_ref=dst,
            send_sem=sems.at[0],
            recv_sem=sems.at[1],
            device_id=(pix_peer(p), site_peer(z)),
            device_id_type=MESH,
        ).start()

    def drain(buffer, sem):
        part = buffer.at[pl.ds(0, buffer.shape[0] - 1)]
        pltpu.make_async_copy(part, part, sem).wait()

    def share_duals(i, values):
        dual_all[i, pl.ds(me, 1)] = values.astype(jnp.bfloat16)[None]

    def send_duals(i):
        for p in range(1, npix):
            send(dual_all.at[i, me], dual_all.at[i, me], dual_sem.at[i], p, 0)

    for copy in small:
        copy.wait()
    share_duals(0, dual_ref[...])

    diagonal = lax.broadcasted_iota(jnp.int32, (slots, slots), 0) == lax.broadcasted_iota(
        jnp.int32, (slots, slots), 1
    )
    pos = jnp.sum(
        jnp.where(diagonal, pos_ref[...].astype(jnp.float32), 0.0), axis=1, keepdims=True
    )
    slot_col = lax.broadcasted_iota(jnp.int32, (slots, 1), 0)
    first = ((slot_col // cap) * rows).astype(jnp.float32)
    base = jnp.where(pos >= 0.0, first + pos * halves, -1.0 * halves)
    row_id = lax.broadcasted_iota(jnp.int32, (slots, npix * rows), 1).astype(jnp.float32)
    choosers = [
        jnp.where(row_id == base + h, 1.0, 0.0).astype(jnp.bfloat16) for h in range(halves)
    ]
    pos_rows = jnp.broadcast_to(pos, (slots, LANES))
    for t in range(npix):
        row_send[t, halves * cap :, :] = pos_rows[t * cap : (t + 1) * cap]
    filled = jnp.broadcast_to(jnp.where(pos >= 0.0, 1.0, 0.0), (slots, width))
    slot_row = lax.broadcasted_iota(jnp.int32, (slots, width), 0) // cap
    slot_lane = lax.broadcasted_iota(jnp.int32, (slots, LANES), 0) % cap

    def of_target(t, values):
        return jnp.where(slot_row == t, values, 0.0).astype(jnp.bfloat16)

    def column_fold(sums):
        total = jnp.zeros((1, LANES), jnp.float32)
        for c in range(cap):
            part = sums[:, c * LANES : (c + 1) * LANES]
            total = total + jnp.sum(jnp.where(slot_lane == c, part, 0.0), axis=0, keepdims=True)
        return total

    lane_row = lax.broadcasted_iota(jnp.int32, (16, cap * LANES), 0)
    lane_cap = lax.broadcasted_iota(jnp.int32, (16, cap * LANES), 1) // LANES

    def spread_sites(values):
        wide = jnp.concatenate([values] * cap, axis=1)
        return jnp.where(lane_row == lane_cap, wide, 0.0).astype(jnp.bfloat16)

    chooser = (
        lax.broadcasted_iota(jnp.int32, (gain_ref.shape[0], sites), 0) == ids_ref[...]
    ).astype(jnp.float32)
    gain_half = 0.5 * lax.dot_general(
        gain_ref[...],
        chooser,
        (((0,), (0,)), ((), ())),
        precision=lax.Precision.HIGHEST,
        preferred_element_type=jnp.float32,
    )

    pl.semaphore_wait(barrier, len(peers))
    send_duals(0)

    def build(t, carry):
        margin_copy(t).wait()
        for c in range(cap):
            part = slice(c * LANES, (c + 1) * LANES)
            values = margins_v[t * cap + c].astype(jnp.float32)
            values = 0.5 * jnp.tanh(values * (0.5 * MARGIN_SCALE) + gain_half) + 0.5
            values = values.astype(jnp.bfloat16)
            tiles[t, :, part] = values
        return carry

    lax.fori_loop(0, npix, build, 0)

    order = list(range(1, npix)) + [0]

    def multiply(lhs, t):
        return jnp.dot(lhs, tiles_t[t], preferred_element_type=jnp.float32)

    def put(target, t, products):
        for h in range(halves):
            target[t, h * cap : (h + 1) * cap, :] = products[:cap, h * LANES : (h + 1) * LANES]

    def send_lines(source, target, sems, arrival, p):
        t = pix_peer(p)
        for z in far_first:
            if p or z:
                pltpu.make_async_remote_copy(
                    src_ref=source.at[t],
                    dst_ref=target.at[mine],
                    send_sem=sems.at[0],
                    recv_sem=arrival,
                    device_id=(t, site_peer(z)),
                    device_id_type=MESH,
                ).start()

    def send_products(values, source, target, sems):
        lhs = spread_sites(values)
        ready = multiply(lhs, pix_peer(order[0]))
        for n, p in enumerate(order):
            put(source, pix_peer(p), ready)
            if n + 1 < npix:
                ready = multiply(lhs, pix_peer(order[n + 1]))
            send_lines(source, target, sems, sems.at[1 + here], p)
        target[pl.ds(mine, 1)] = source[pl.ds(me, 1)]

    lhs = spread_sites(jnp.ones((1, LANES), jnp.float32))
    for t in range(npix):
        tiles_t[t] = tiles[t].T
        put(row_send, t, multiply(lhs, t))
    for p in range(1, npix):
        send(row_send.at[pix_peer(p)], row_recv.at[me], row_sem, p, 0)
    row_recv[pl.ds(me, 1)] = row_send[pl.ds(me, 1)]

    state_row = lax.broadcasted_iota(jnp.int32, (rows, LANES), 0).astype(jnp.float32)

    def gather_group(z, buffer, first_line):
        total = jnp.zeros((rows, LANES), jnp.float32)
        for p in range(npix):
            for c in range(cap):
                at = rows + p * cap + c
                offset = state_row - level_recv[z, at : at + 1, :] * halves
                for h in range(halves):
                    line = buffer[first_line + p, h * cap + c : h * cap + c + 1, :]
                    total = total + jnp.where(offset == h, line, 0.0)
        return total

    def gather_rows(buffer, arrivals):
        def wait_for(z, count):
            part = buffer.at[pl.ds(z * npix, count)]
            pltpu.make_async_copy(part, part, arrivals.at[1 + z]).wait()

        wait_for(here, npix - 1)
        parts[here] = gather_group(here, buffer, here * npix)

        @pl.loop(1, nsite)
        def others(step):
            z = lax.rem(here + step, nsite)
            wait_for(z, npix)
            parts[z] = gather_group(z, buffer, z * npix)

        total = parts[0]
        for z in range(1, nsite):
            total = total + parts[z]
        return total

    site_level = site_ref[...]
    pixel_level = pixel_ref[...]
    duals = dual_ref[...]
    column_sum = None
    row_sum = None
    for i in range(ITERS):
        drain(dual_all.at[i], dual_sem.at[i, 1])
        all_rows = dual_all[i].reshape(npix * rows, LANES)
        selected = jnp.concatenate(
            [jnp.dot(ch, all_rows, preferred_element_type=jnp.float32) for ch in choosers], axis=1
        )
        groups = [selected, filled] if i == 0 else [selected]
        sums = jnp.zeros((len(groups) * slots, cap * LANES), jnp.float32)
        for t in range(npix):
            lhs = jnp.concatenate([of_target(t, group) for group in groups], axis=0)
            sums = sums + jnp.dot(lhs, tiles[t], preferred_element_type=jnp.float32)
        for n in range(len(groups)):
            total = column_fold(sums[n * slots : (n + 1) * slots])
            col_recv[i, pl.ds(me, 1), n : n + 1] = total[None]
        for p in range(1, npix):
            send(col_recv.at[i, me], col_recv.at[i, me], col_sem.at[i], p, 0)

        new_pixel = jnp.clip(pixel_level - (duals - weights_ref[...]), 0.0, 1.0)
        ahead = 2.0 * new_pixel - pixel_level
        if i == 0:
            drain(row_recv, row_sem.at[1])
            for p in range(npix):
                at = rows + p * cap
                level_recv[here, at : at + cap, :] = row_recv[p, halves * cap :, :]
            level_recv[here, :rows, :] = gather_group(here, row_recv, 0)
            for z in far_first:
                if z:
                    send(level_recv.at[here], level_recv.at[here], level_sem, 0, z)

        drain(col_recv.at[i], col_sem.at[i, 1])
        pulled = col_recv[i, 0]
        for s in range(1, npix):
            pulled = pulled + col_recv[i, s]
        if i == 0:
            column_sum = pulled[1:2]
        new_site = jnp.clip(site_level - (price_ref[...] - pulled[0:1] / column_sum), 0.0, 1.0)
        send_products(
            2.0 * new_site - site_level, push_send.at[i], push_recv.at[i], push_sem.at[i]
        )
        if i == 0:
            drain(level_recv, level_sem.at[1])
            row_sum = level_recv[0, :rows, :]
            for z in range(1, nsite):
                row_sum = row_sum + level_recv[z, :rows, :]
            row_sum = row_sum + 1.0
        pushed = gather_rows(push_recv.at[i], push_sem.at[i])
        duals = jnp.maximum(duals + (ahead - pushed) / row_sum, 0.0)
        if i < ITERS - 1:
            share_duals(i + 1, duals)
            send_duals(i + 1)
        site_level, pixel_level = new_site, new_pixel

    site_out[...] = site_level
    pixel_out[...] = pixel_level
    dual_out[...] = duals
    move_all(
        (site_out, pixel_out, dual_out),
        (site_hbm_out, pixel_hbm_out, dual_hbm_out),
        small_sem,
    )

    drain(row_recv, row_sem.at[0])
    drain(level_recv, level_sem.at[0])
    for i in range(ITERS):
        drain(dual_all.at[i], dual_sem.at[i, 0])
        drain(col_recv.at[i], col_sem.at[i, 0])
        drain(push_recv.at[i], push_sem.at[i, 0])


def move_all(sources, targets, sem):
    copies = [
        pltpu.make_async_copy(src, dst, sem.at[n])
        for n, (src, dst) in enumerate(zip(sources, targets))
    ]
    for copy in copies:
        copy.start()
    for copy in copies:
        copy.wait()


def hand_on(site_in, pixel_in, dual_in, site_out, pixel_out, dual_out, site, pixel, dual, sem):
    held = (site, pixel, dual)
    move_all((site_in, pixel_in, dual_in), held, sem)
    move_all(held, (site_out, pixel_out, dual_out), sem)


def local(
    npix,
    nsite,
    margins,
    block_pos,
    pattern_ids,
    pattern_gain,
    site_price,
    weights,
    site_start,
    pixel_start,
    dual_start,
):
    slots, width, sites = margins.shape
    cap = slots // npix
    halves = width // LANES
    rows = weights.shape[0] // LANES
    devices = npix * nsite
    f32 = jnp.float32
    i32 = jnp.int32
    hbm = pl.BlockSpec(memory_space=pltpu.HBM)
    dma = pltpu.SemaphoreType.DMA
    results = (
        jax.ShapeDtypeStruct((1, sites), f32),
        jax.ShapeDtypeStruct((rows, LANES), f32),
        jax.ShapeDtypeStruct((rows, LANES), f32),
    )
    found = pl.pallas_call(
        functools.partial(kernel, npix, nsite),
        out_shape=results,
        in_specs=[hbm] * 9,
        out_specs=(hbm, hbm, hbm),
        scratch_shapes=[
            pltpu.VMEM((1, sites), f32),
            pltpu.VMEM((rows, LANES), f32),
            pltpu.VMEM((rows, LANES), f32),
            pltpu.VMEM((slots, width, sites), i32),
            pltpu.VMEM((1, slots), i32),
            pltpu.VMEM((1, sites), i32),
            pltpu.VMEM(pattern_gain.shape, f32),
            pltpu.VMEM((1, sites), f32),
            pltpu.VMEM((rows, LANES), f32),
            pltpu.VMEM((1, sites), f32),
            pltpu.VMEM((rows, LANES), f32),
            pltpu.VMEM((rows, LANES), f32),
            pltpu.VMEM((npix, width, cap * sites), jnp.bfloat16),
            pltpu.VMEM((npix, cap * sites, width), jnp.bfloat16),
            pltpu.VMEM((ITERS, npix, rows, LANES), jnp.bfloat16),
            pltpu.VMEM((npix, (halves + 1) * cap, LANES), f32),
            pltpu.VMEM((npix, (halves + 1) * cap, LANES), f32),
            pltpu.VMEM((ITERS, npix, 2, LANES), f32),
            pltpu.VMEM((ITERS, npix, halves * cap, LANES), f32),
            pltpu.VMEM((ITERS, devices, halves * cap, LANES), f32),
            pltpu.VMEM((nsite, rows, LANES), f32),
            pltpu.VMEM((nsite, rows + slots, LANES), f32),
            dma((2,)),
            dma((npix,)),
            dma((8,)),
            dma((ITERS, 2)),
            dma((2,)),
            dma((ITERS, 2)),
            dma((ITERS, 1 + nsite)),
        ],
        compiler_params=pltpu.CompilerParams(
            collective_id=0, has_side_effects=True, vmem_limit_bytes=60 * 1024 * 1024
        ),
    )(
        margins,
        block_pos.reshape(1, slots),
        pattern_ids.reshape(1, sites),
        pattern_gain,
        site_price.reshape(1, sites),
        weights.reshape(rows, LANES),
        site_start.reshape(1, sites),
        pixel_start.reshape(rows, LANES),
        dual_start.reshape(rows, LANES),
    )
    site_level, pixel_level, duals = pl.pallas_call(
        hand_on,
        out_shape=results,
        in_specs=[hbm] * 3,
        out_specs=(hbm, hbm, hbm),
        scratch_shapes=[pltpu.VMEM(r.shape, f32) for r in results] + [dma((3,))],
        compiler_params=pltpu.CompilerParams(vmem_limit_bytes=60 * 1024 * 1024),
    )(*found)
    return site_level.reshape(-1), pixel_level.reshape(-1), duals.reshape(-1)


def solution(mesh):
    placed = (
        P("pix", None, "site"),
        P("pix", "site"),
        P("site"),
        P(),
        P("site"),
        P("pix"),
        P("site"),
        P("pix"),
        P("pix"),
    )
    return jax.shard_map(
        functools.partial(local, mesh.shape["pix"], mesh.shape["site"]),
        mesh=mesh,
        in_specs=placed,
        out_specs=(P("site"), P("pix"), P("pix")),
        check_vma=False,
    )
```

```python
import functools

import jax
import jax.numpy as jnp
from jax import lax
from jax.experimental import pallas as pl
from jax.experimental.pallas import tpu as pltpu
from jax.sharding import PartitionSpec as P

ITERS = 2
MARGIN_SCALE = 2.0 ** (-9)
LANES = 128
MESH = pl.DeviceIdType.MESH


def kernel(
    npix,
    nsite,
    margins_hbm,
    pos_hbm,
    ids_hbm,
    gain_hbm,
    price_hbm,
    weights_hbm,
    site_hbm,
    pixel_hbm,
    dual_hbm,
    site_hbm_out,
    pixel_hbm_out,
    dual_hbm_out,
    site_out,
    pixel_out,
    dual_out,
    margins_v,
    pos_ref,
    ids_ref,
    gain_ref,
    price_ref,
    weights_ref,
    site_ref,
    pixel_ref,
    dual_ref,
    tiles,
    tiles_t,
    dual_all,
    row_send,
    row_recv,
    col_recv,
    push_send,
    push_recv,
    parts,
    level_recv,
    level_sem,
    margin_sem,
    small_sem,
    dual_sem,
    row_sem,
    col_sem,
    push_sem,
):
    slots, width, sites = margins_v.shape
    cap = slots // npix
    halves = width // LANES
    rows = dual_ref.shape[0]
    me = lax.axis_index("pix")
    here = lax.axis_index("site")
    mine = here * npix + me

    pix_ids = [me] + [lax.rem(me + step, npix) for step in range(1, npix)]
    site_ids = [here] + [lax.rem(here + step, nsite) for step in range(1, nsite)]

    def pix_peer(step):
        return pix_ids[step]

    def site_peer(step):
        return site_ids[step]

    far_first = sorted(range(nsite), key=lambda z: -min(z, nsite - z))
    peers = [(p, z) for p in list(range(1, npix)) + [0] for z in far_first if p or z]

    small = [
        pltpu.make_async_copy(src, dst, small_sem.at[n])
        for n, (src, dst) in enumerate(
            (
                (dual_hbm, dual_ref),
                (pos_hbm, pos_ref),
                (ids_hbm, ids_ref),
                (gain_hbm, gain_ref),
                (price_hbm, price_ref),
                (weights_hbm, weights_ref),
                (site_hbm, site_ref),
                (pixel_hbm, pixel_ref),
            )
        )
    ]

    def margin_copy(t):
        part = pl.ds(t * cap, cap)
        return pltpu.make_async_copy(margins_hbm.at[part], margins_v.at[part], margin_sem.at[t])

    barrier = pltpu.get_barrier_semaphore()
    for p, z in peers:
        pl.semaphore_signal(
            barrier, inc=1, device_id=(pix_peer(p), site_peer(z)), device_id_type=MESH
        )

    for copy in small:
        copy.start()
    for t in range(npix):
        margin_copy(t).start()

    def send(src, dst, sems, p, z):
        pltpu.make_async_remote_copy(
            src_ref=src,
            dst_ref=dst,
            send_sem=sems.at[0],
            recv_sem=sems.at[1],
            device_id=(pix_peer(p), site_peer(z)),
            device_id_type=MESH,
        ).start()

    def drain(buffer, sem):
        part = buffer.at[pl.ds(0, buffer.shape[0] - 1)]
        pltpu.make_async_copy(part, part, sem).wait()

    def share_duals(i, values):
        dual_all[i, pl.ds(me, 1)] = values.astype(jnp.bfloat16)[None]

    def send_duals(i):
        for p in range(1, npix):
            send(dual_all.at[i, me], dual_all.at[i, me], dual_sem.at[i], p, 0)

    for copy in small:
        copy.wait()
    share_duals(0, dual_ref[...])

    diagonal = lax.broadcasted_iota(jnp.int32, (slots, slots), 0) == lax.broadcasted_iota(
        jnp.int32, (slots, slots), 1
    )
    pos = jnp.sum(
        jnp.where(diagonal, pos_ref[...].astype(jnp.float32), 0.0), axis=1, keepdims=True
    )
    slot_col = lax.broadcasted_iota(jnp.int32, (slots, 1), 0)
    first = ((slot_col // cap) * rows).astype(jnp.float32)
    base = jnp.where(pos >= 0.0, first + pos * halves, -1.0 * halves)
    row_id = lax.broadcasted_iota(jnp.int32, (slots, npix * rows), 1).astype(jnp.float32)
    choosers = [
        jnp.where(row_id == base + h, 1.0, 0.0).astype(jnp.bfloat16) for h in range(halves)
    ]
    pos_rows = jnp.broadcast_to(pos, (slots, LANES))
    for t in range(npix):
        row_send[t, halves * cap :, :] = pos_rows[t * cap : (t + 1) * cap]
    filled = jnp.broadcast_to(jnp.where(pos >= 0.0, 1.0, 0.0), (slots, width))
    slot_row = lax.broadcasted_iota(jnp.int32, (slots, width), 0) // cap
    slot_lane = lax.broadcasted_iota(jnp.int32, (slots, LANES), 0) % cap

    def of_target(t, values):
        return jnp.where(slot_row == t, values, 0.0).astype(jnp.bfloat16)

    def column_fold(sums):
        total = jnp.zeros((1, LANES), jnp.float32)
        for c in range(cap):
            part = sums[:, c * LANES : (c + 1) * LANES]
            total = total + jnp.sum(jnp.where(slot_lane == c, part, 0.0), axis=0, keepdims=True)
        return total

    lane_row = lax.broadcasted_iota(jnp.int32, (16, cap * LANES), 0)
    lane_cap = lax.broadcasted_iota(jnp.int32, (16, cap * LANES), 1) // LANES

    def spread_sites(values):
        wide = jnp.concatenate([values] * cap, axis=1)
        return jnp.where(lane_row == lane_cap, wide, 0.0).astype(jnp.bfloat16)

    chooser = (
        lax.broadcasted_iota(jnp.int32, (gain_ref.shape[0], sites), 0) == ids_ref[...]
    ).astype(jnp.float32)
    gain_half = 0.5 * lax.dot_general(
        gain_ref[...],
        chooser,
        (((0,), (0,)), ((), ())),
        precision=lax.Precision.HIGHEST,
        preferred_element_type=jnp.float32,
    )

    pl.semaphore_wait(barrier, len(peers))
    send_duals(0)

    def build(t, carry):
        margin_copy(t).wait()
        for c in range(cap):
            part = slice(c * LANES, (c + 1) * LANES)
            values = margins_v[t * cap + c].astype(jnp.float32)
            values = 0.5 * jnp.tanh(values * (0.5 * MARGIN_SCALE) + gain_half) + 0.5
            values = values.astype(jnp.bfloat16)
            tiles[t, :, part] = values
        return carry

    lax.fori_loop(0, npix, build, 0)

    order = list(range(1, npix)) + [0]

    def multiply(lhs, t):
        return jnp.dot(lhs, tiles_t[t], preferred_element_type=jnp.float32)

    def put(target, t, products):
        for h in range(halves):
            target[t, h * cap : (h + 1) * cap, :] = products[:cap, h * LANES : (h + 1) * LANES]

    def send_lines(source, target, sems, arrival, p, sites):
        t = pix_peer(p)
        for z in sites:
            if p or z:
                pltpu.make_async_remote_copy(
                    src_ref=source.at[t],
                    dst_ref=target.at[mine],
                    send_sem=sems.at[0],
                    recv_sem=arrival,
                    device_id=(t, site_peer(z)),
                    device_id_type=MESH,
                ).start()

    def send_products(values, source, target, sems):
        lhs = spread_sites(values)
        ready = multiply(lhs, pix_peer(order[0]))
        for n, p in enumerate(order):
            put(source, pix_peer(p), ready)
            if n + 1 < npix:
                ready = multiply(lhs, pix_peer(order[n + 1]))
            send_lines(source, target, sems, sems.at[1 + here], p, far_first[:1])
        for z in far_first[1:]:
            for p in order:
                send_lines(source, target, sems, sems.at[1 + here], p, [z])
        target[pl.ds(mine, 1)] = source[pl.ds(me, 1)]

    lhs = spread_sites(jnp.ones((1, LANES), jnp.float32))
    for t in range(npix):
        tiles_t[t] = tiles[t].T
        put(row_send, t, multiply(lhs, t))
    for p in range(1, npix):
        send(row_send.at[pix_peer(p)], row_recv.at[me], row_sem, p, 0)
    row_recv[pl.ds(me, 1)] = row_send[pl.ds(me, 1)]

    state_row = lax.broadcasted_iota(jnp.int32, (rows, LANES), 0).astype(jnp.float32)

    def gather_group(z, buffer, first_line):
        total = jnp.zeros((rows, LANES), jnp.float32)
        for p in range(npix):
            for c in range(cap):
                at = rows + p * cap + c
                offset = state_row - level_recv[z, at : at + 1, :] * halves
                for h in range(halves):
                    line = buffer[first_line + p, h * cap + c : h * cap + c + 1, :]
                    total = total + jnp.where(offset == h, line, 0.0)
        return total

    def gather_rows(buffer, arrivals):
        def wait_for(z, count):
            part = buffer.at[pl.ds(z * npix, count)]
            pltpu.make_async_copy(part, part, arrivals.at[1 + z]).wait()

        wait_for(here, npix - 1)
        parts[here] = gather_group(here, buffer, here * npix)

        @pl.loop(1, nsite)
        def others(step):
            z = lax.rem(here + step, nsite)
            wait_for(z, npix)
            parts[z] = gather_group(z, buffer, z * npix)

        total = parts[0]
        for z in range(1, nsite):
            total = total + parts[z]
        return total

    site_level = site_ref[...]
    pixel_level = pixel_ref[...]
    duals = dual_ref[...]
    column_sum = None
    row_sum = None
    for i in range(ITERS):
        drain(dual_all.at[i], dual_sem.at[i, 1])
        all_rows = dual_all[i].reshape(npix * rows, LANES)
        selected = jnp.concatenate(
            [jnp.dot(ch, all_rows, preferred_element_type=jnp.float32) for ch in choosers], axis=1
        )
        groups = [selected, filled] if i == 0 else [selected]
        sums = jnp.zeros((len(groups) * slots, cap * LANES), jnp.float32)
        for t in range(npix):
            lhs = jnp.concatenate([of_target(t, group) for group in groups], axis=0)
            sums = sums + jnp.dot(lhs, tiles[t], preferred_element_type=jnp.float32)
        for n in range(len(groups)):
            total = column_fold(sums[n * slots : (n + 1) * slots])
            col_recv[i, pl.ds(me, 1), n : n + 1] = total[None]
        for p in range(1, npix):
            send(col_recv.at[i, me], col_recv.at[i, me], col_sem.at[i], p, 0)

        new_pixel = jnp.clip(pixel_level - (duals - weights_ref[...]), 0.0, 1.0)
        ahead = 2.0 * new_pixel - pixel_level
        if i == 0:
            drain(row_recv, row_sem.at[1])
            for p in range(npix):
                at = rows + p * cap
                level_recv[here, at : at + cap, :] = row_recv[p, halves * cap :, :]
            level_recv[here, :rows, :] = gather_group(here, row_recv, 0)
            for z in far_first:
                if z:
                    send(level_recv.at[here], level_recv.at[here], level_sem, 0, z)

        drain(col_recv.at[i], col_sem.at[i, 1])
        pulled = col_recv[i, 0]
        for s in range(1, npix):
            pulled = pulled + col_recv[i, s]
        if i == 0:
            column_sum = pulled[1:2]
        new_site = jnp.clip(site_level - (price_ref[...] - pulled[0:1] / column_sum), 0.0, 1.0)
        send_products(
            2.0 * new_site - site_level, push_send.at[i], push_recv.at[i], push_sem.at[i]
        )
        if i == 0:
            drain(level_recv, level_sem.at[1])
            row_sum = level_recv[0, :rows, :]
            for z in range(1, nsite):
                row_sum = row_sum + level_recv[z, :rows, :]
            row_sum = row_sum + 1.0
        pushed = gather_rows(push_recv.at[i], push_sem.at[i])
        duals = jnp.maximum(duals + (ahead - pushed) / row_sum, 0.0)
        if i < ITERS - 1:
            share_duals(i + 1, duals)
            send_duals(i + 1)
        site_level, pixel_level = new_site, new_pixel

    site_out[...] = site_level
    pixel_out[...] = pixel_level
    dual_out[...] = duals
    move_all(
        (site_out, pixel_out, dual_out),
        (site_hbm_out, pixel_hbm_out, dual_hbm_out),
        small_sem,
    )

    drain(row_recv, row_sem.at[0])
    drain(level_recv, level_sem.at[0])
    for i in range(ITERS):
        drain(dual_all.at[i], dual_sem.at[i, 0])
        drain(col_recv.at[i], col_sem.at[i, 0])
        drain(push_recv.at[i], push_sem.at[i, 0])


def move_all(sources, targets, sem):
    copies = [
        pltpu.make_async_copy(src, dst, sem.at[n])
        for n, (src, dst) in enumerate(zip(sources, targets))
    ]
    for copy in copies:
        copy.start()
    for copy in copies:
        copy.wait()


def hand_on(site_in, pixel_in, dual_in, site_out, pixel_out, dual_out, site, pixel, dual, sem):
    held = (site, pixel, dual)
    move_all((site_in, pixel_in, dual_in), held, sem)
    move_all(held, (site_out, pixel_out, dual_out), sem)


def local(
    npix,
    nsite,
    margins,
    block_pos,
    pattern_ids,
    pattern_gain,
    site_price,
    weights,
    site_start,
    pixel_start,
    dual_start,
):
    slots, width, sites = margins.shape
    cap = slots // npix
    halves = width // LANES
    rows = weights.shape[0] // LANES
    devices = npix * nsite
    f32 = jnp.float32
    i32 = jnp.int32
    hbm = pl.BlockSpec(memory_space=pltpu.HBM)
    dma = pltpu.SemaphoreType.DMA
    results = (
        jax.ShapeDtypeStruct((1, sites), f32),
        jax.ShapeDtypeStruct((rows, LANES), f32),
        jax.ShapeDtypeStruct((rows, LANES), f32),
    )
    found = pl.pallas_call(
        functools.partial(kernel, npix, nsite),
        out_shape=results,
        in_specs=[hbm] * 9,
        out_specs=(hbm, hbm, hbm),
        scratch_shapes=[
            pltpu.VMEM((1, sites), f32),
            pltpu.VMEM((rows, LANES), f32),
            pltpu.VMEM((rows, LANES), f32),
            pltpu.VMEM((slots, width, sites), i32),
            pltpu.VMEM((1, slots), i32),
            pltpu.VMEM((1, sites), i32),
            pltpu.VMEM(pattern_gain.shape, f32),
            pltpu.VMEM((1, sites), f32),
            pltpu.VMEM((rows, LANES), f32),
            pltpu.VMEM((1, sites), f32),
            pltpu.VMEM((rows, LANES), f32),
            pltpu.VMEM((rows, LANES), f32),
            pltpu.VMEM((npix, width, cap * sites), jnp.bfloat16),
            pltpu.VMEM((npix, cap * sites, width), jnp.bfloat16),
            pltpu.VMEM((ITERS, npix, rows, LANES), jnp.bfloat16),
            pltpu.VMEM((npix, (halves + 1) * cap, LANES), f32),
            pltpu.VMEM((npix, (halves + 1) * cap, LANES), f32),
            pltpu.VMEM((ITERS, npix, 2, LANES), f32),
            pltpu.VMEM((ITERS, npix, halves * cap, LANES), f32),
            pltpu.VMEM((ITERS, devices, halves * cap, LANES), f32),
            pltpu.VMEM((nsite, rows, LANES), f32),
            pltpu.VMEM((nsite, rows + slots, LANES), f32),
            dma((2,)),
            dma((npix,)),
            dma((8,)),
            dma((ITERS, 2)),
            dma((2,)),
            dma((ITERS, 2)),
            dma((ITERS, 1 + nsite)),
        ],
        compiler_params=pltpu.CompilerParams(
            collective_id=0, has_side_effects=True, vmem_limit_bytes=60 * 1024 * 1024
        ),
    )(
        margins,
        block_pos.reshape(1, slots),
        pattern_ids.reshape(1, sites),
        pattern_gain,
        site_price.reshape(1, sites),
        weights.reshape(rows, LANES),
        site_start.reshape(1, sites),
        pixel_start.reshape(rows, LANES),
        dual_start.reshape(rows, LANES),
    )
    site_level, pixel_level, duals = pl.pallas_call(
        hand_on,
        out_shape=results,
        in_specs=[hbm] * 3,
        out_specs=(hbm, hbm, hbm),
        scratch_shapes=[pltpu.VMEM(r.shape, f32) for r in results] + [dma((3,))],
        compiler_params=pltpu.CompilerParams(vmem_limit_bytes=60 * 1024 * 1024),
    )(*found)
    return site_level.reshape(-1), pixel_level.reshape(-1), duals.reshape(-1)


def solution(mesh):
    placed = (
        P("pix", None, "site"),
        P("pix", "site"),
        P("site"),
        P(),
        P("site"),
        P("pix"),
        P("site"),
        P("pix"),
        P("pix"),
    )
    return jax.shard_map(
        functools.partial(local, mesh.shape["pix"], mesh.shape["site"]),
        mesh=mesh,
        in_specs=placed,
        out_specs=(P("site"), P("pix"), P("pix")),
        check_vma=False,
    )
```
